128 devices in a mesh: gx: 4 (over x), gy: 32 (over z, y, core).
Axes of the slice: x: 4, y: 4, z: 4, core: 2. Of those that a mesh axis runs over, the one named last changes fastest.
Arguments:
- fields: float32 [256, 6, 32, 1024], P(('gx', 'gy')), may hold values from -6 to 6
- speeds: float32 [256, 3, 32, 1024], P(('gx', 'gy')), may hold values from -0.4 to 0.4
- neighbours: int32 [256, 6], replicated, may hold values from -1 to 255, as said below
- block_order: int32 [256], replicated, may hold values from 0 to 255, as said below
- tiles: float32 [16384, 8, 128], P(('gx', 'gy')), may hold values from -6 to 6
- tile_fill: int32 [16384], P(('gx', 'gy')), may hold values from 1 to 128
- tile_dest: int32 [16384, 1], P(('gx', 'gy')), may hold values from 0 to 127; in each aligned block of 128 rows (0 to 127, 128 to 255, ...) at most 2 rows name the same one
Outputs:
- blocks_out: float32 [256, 6, 32, 1024], P(('gx', 'gy'))
- tiles_out: float32 [32768, 8, 128], P(('gx', 'gy'))
- fill_out: int32 [32768], P(('gx', 'gy'))
The draws below stay inside these ranges and needn't reach their ends.
Inputs may be any that keep to these rules, and one draw needn't show every extreme that they name: Entries 2 d and 2 d + 1 of a row name the blocks below and above along direction d, or -1 at the domain's edge; the relation is symmetric; a block b stands on device b // 2, and each of its neighbours on a device at most 2 away. A permutation; block_order[j] // 2 differs from j // 2 by at most 1, and by 1 for some j. `tile_dest`: among the 128 tiles of one device, no destination is named more than 2 times.
All inputs are finite; a program needn't handle non-finite values.
Results may differ from the reference program's by a relative error of at most 0.0003.
Values sent between devices are 32-bit elements; how exact they have to be, the bound alone decides.
A program may use at most 128 MiB of HBM per device.

```python
import math
import jax
import jax.numpy as jnp
import numpy as np
from jax import lax

BS = 32
NF = 6
NA = 8
TR = 128
CAPT = 2
NEAR = 2
BLK_DEV = 2
TILES_DEV = 128
BLOCKS = 256
TILES = 16384
N_GX = 4
N_GY = 32
DEVICES = 128


def draw_block_order(key, part):
    identity = jnp.arange(BLOCKS, dtype=jnp.int32)
    lifted = jax.random.randint(jax.random.fold_in(key, 11), (BLOCKS,), 0, BLK_DEV + 1).astype(jnp.int32)
    second = (identity >= BLK_DEV) & (identity < 2 * BLK_DEV)
    lifted = jnp.where(second, 0, lifted)
    lifted = jnp.where(identity == BLK_DEV - 1, BLK_DEV, lifted)
    scores = (identity + lifted) * BLOCKS + (BLOCKS - 1 - identity)
    return jnp.argsort(scores, stable=True).astype(jnp.int32)


def draw_neighbours(key, part):
    plane = BLK_DEV * NEAR
    groups = BLOCKS // BLK_DEV
    depth = BLOCKS // plane
    places = jnp.arange(BLOCKS, dtype=jnp.int32)
    coord_x = places // plane
    coord_y = places % plane // BLK_DEV
    coord_z = places % BLK_DEV
    scores = jax.random.randint(jax.random.fold_in(key, 21), (groups, BLK_DEV), 0, 1 << 20).astype(jnp.int32)
    scores = scores * BLK_DEV + jnp.arange(BLK_DEV, dtype=jnp.int32)[None, :]
    shuffle = jnp.argsort(scores, axis=1, stable=True).astype(jnp.int32)
    holder = (jnp.arange(groups, dtype=jnp.int32)[:, None] * BLK_DEV + shuffle).reshape(-1)

    def site_of(left, middle, right):
        return left * plane + middle * BLK_DEV + right
    lattice = jnp.stack([jnp.where(coord_x > 0, holder[site_of(jnp.maximum(coord_x - 1, 0), coord_y, coord_z)], -1), jnp.where(coord_x < depth - 1, holder[site_of(jnp.minimum(coord_x + 1, depth - 1), coord_y, coord_z)], -1), holder[site_of(coord_x, (coord_y + NEAR - 1) % NEAR, coord_z)], holder[site_of(coord_x, (coord_y + 1) % NEAR, coord_z)], holder[site_of(coord_x, coord_y, (coord_z + BLK_DEV - 1) % BLK_DEV)], holder[site_of(coord_x, coord_y, (coord_z + 1) % BLK_DEV)]], axis=1)
    flips = jax.random.randint(jax.random.fold_in(key, 22), (3,), 0, 2).astype(jnp.int32)
    turn_scores = jax.random.randint(jax.random.fold_in(key, 23), (3,), 0, 1 << 20).astype(jnp.int32) * 3 + jnp.arange(3, dtype=jnp.int32)
    turning = jnp.argsort(turn_scores, stable=True).astype(jnp.int32)
    columns = []
    for direction in range(3):
        lattice_axis = turning[direction]
        low_side = jnp.take(lattice, 2 * lattice_axis, axis=1)
        high_side = jnp.take(lattice, 2 * lattice_axis + 1, axis=1)
        flipped = flips[lattice_axis] == 1
        columns.append(jnp.where(flipped, high_side, low_side))
        columns.append(jnp.where(flipped, low_side, high_side))
    table = jnp.stack(columns, axis=1).astype(jnp.int32)
    return jnp.zeros((BLOCKS, 6), jnp.int32).at[holder].set(table)


def with_ends(values, own_key, smallest, top_value):
    dims = values.shape
    index_at = [jax.random.randint(jax.random.fold_in(own_key, axis), (), 0, dims[axis]) for axis in range(len(dims))]
    values = values.at[tuple(index_at)].set(smallest)
    longest = dims.index(max(dims))
    index_at[longest] = (index_at[longest] + 1) % dims[longest]
    return values.at[tuple(index_at)].set(top_value)


def block_levels(rng, shape, cuts, low, high):
    def one(axis_at, parts):
        steps = jax.random.uniform(jax.random.fold_in(jax.random.fold_in(rng, 6), axis_at), (parts,), jnp.float32, low / len(cuts), high / len(cuts))
        return jnp.repeat(jnp.exp(steps), shape[axis_at] // parts).reshape((-1,) + (1,) * (len(shape) - axis_at - 1))

    loudness = one(*cuts[0])
    for cut in cuts[1:]:
        loudness = loudness * one(*cut)
    return loudness


def routed_block(stream_key, own, number, rows, amount, top, reach, slope):
    sequence = jax.random.permutation(stream_key, amount)
    crowded, common = portions_of(amount, rows * top, reach, slope, True), portions_of(amount, rows * top, reach, slope, False)
    places = jnp.arange(amount)

    def named(sizes, rotation):
        used = int((sizes > 0).sum())
        fixed = max(1, used // 4)
        passed = fixed + (places - fixed + rotation * (used - fixed)) % max(1, amount - fixed)
        return jnp.zeros((amount,), jnp.int32).at[sequence[jnp.where(places < fixed, places, passed)]].set(jnp.asarray(sizes, jnp.int32))

    sizes = jnp.where(number % 4 == 0, named(crowded, number // 4), named(common, number - number // 4 - 1))
    mixed = jax.random.permutation(jax.random.fold_in(own, 3), amount)
    donor, sink = mixed[0:amount // 2 * 2:2], mixed[1:amount // 2 * 2:2]
    slack = jnp.minimum(sizes[donor] - 1, reach - sizes[sink]) // 2
    slack = jnp.where((donor == sequence[0]) | (sink == sequence[0]) | (sizes[sink] == 0), 0, jnp.maximum(slack, 0))
    passed = jax.random.randint(jax.random.fold_in(own, 4), (amount // 2,), 0, 1 << 20) % (slack + 1)
    sizes = sizes.at[donor].add(-passed).at[sink].add(passed)
    members = jnp.searchsorted(jnp.cumsum(sizes), jnp.arange(rows * top), side="right").astype(jnp.int32)
    table = members.reshape(top, rows).T
    table = table[jax.random.permutation(jax.random.fold_in(own, 1), rows)]
    rotation = jax.random.randint(jax.random.fold_in(own, 2), (rows, 1), 0, top)
    return jnp.take_along_axis(table, (jnp.arange(top)[None, :] + rotation) % top, axis=1)


def portions_of(count, total, most, slope, full):
    loads = [(1 << 20) // math.isqrt(rank ** slope) + 1 for rank in range(1, count + 1)]
    largest = most if full else min(most, max(-(-total // count), total * loads[0] // sum(loads)))
    least = 1 if total - largest >= count - 1 else 0
    given, spare = [largest] + [least] * (count - 1), total - largest - least * (count - 1)
    while spare > 0:
        candidates = [i for i in range(1, count) if given[i] < largest] or [i for i in range(1, count) if given[i] < most]
        pool, budget = sum([loads[i] for i in candidates]), spare
        for i in candidates:
            more = min(most - given[i], max(1, budget * loads[i] // pool), spare)
            given[i] = given[i] + more
            spare = spare - more
    return np.array(given)


def bell_draw(rng, extent, deviation, most, shards=(), kind=jnp.bfloat16):
    result = deviation * jax.random.normal(rng, extent, jnp.float32)
    if shards:
        result = result * block_levels(rng, extent, shards, -0.22, 0.18)
    return jnp.clip(result, -most, most).astype(kind)


def setup_inputs(seed: int = 0) -> dict:
    arg_keys = jax.random.split(jax.random.key(seed), 8)
    fields = bell_draw(arg_keys[0], (BLOCKS, NF, BS, BS * BS), 1.0, 6.0, ((0, 128),), jnp.float32)
    speeds = jnp.clip(jax.random.uniform(arg_keys[1], (BLOCKS, 3, BS, BS * BS), jnp.float32, -0.4, 0.4) * block_levels(arg_keys[1], (BLOCKS, 3, BS, BS * BS), ((0, 128),), -0.4, 0.0), -0.4, 0.4)
    neighbours = draw_neighbours(jax.random.fold_in(arg_keys[7], 71), 0)
    block_order = draw_block_order(jax.random.fold_in(arg_keys[7], 71), 0)
    tiles = bell_draw(arg_keys[4], (TILES, NA, TR), 1.0, 6.0, ((0, 128),), jnp.float32)
    tile_fill = with_ends(jax.random.randint(arg_keys[5], (TILES,), 1, TR + 1), jax.random.fold_in(arg_keys[5], 1), 1, TR).astype(jnp.int32)
    tile_dest_keys = jax.random.split(jax.random.fold_in(arg_keys[6], 1), TILES // TILES_DEV)
    tile_dest_turns = jax.random.permutation(jax.random.fold_in(arg_keys[6], 3), TILES // TILES_DEV)
    tile_dest = jax.vmap(lambda own, number: routed_block(jax.random.fold_in(arg_keys[6], 2), own, number, TILES_DEV, DEVICES, 1, CAPT, 2))(tile_dest_keys, tile_dest_turns).reshape((TILES, 1))
    return dict(fields=fields, speeds=speeds, neighbours=neighbours, block_order=block_order, tiles=tiles, tile_fill=tile_fill, tile_dest=tile_dest)


DRIFT = 0.5


def directional(values, velocity, direction):
    width = values.shape[2]
    joined = jnp.concatenate([values, velocity[:, direction:direction + 1]], axis=1)
    joined = joined.reshape(joined.shape[0], joined.shape[1], width, width, width)
    joined = jnp.moveaxis(joined, 2 + direction, 2)
    return joined.reshape(joined.shape[0], joined.shape[1], width, width * width)


def restore(swept, direction):
    width = swept.shape[2]
    cube = swept.reshape(swept.shape[0], swept.shape[1], width, width, width)
    cube = jnp.moveaxis(cube, 2, 2 + direction)
    return cube.reshape(swept.shape[0], swept.shape[1], width, width * width)


def face_layers(joined):
    return jnp.stack([joined[:, :, :3], joined[:, :, -3:]], axis=1)


def ppm_update(values, courant):
    width = values.shape[2] - 6
    left_cell = values[:, :, 1:-2]
    right_cell = values[:, :, 2:-1]
    edges = (7.0 / 12.0) * (left_cell + right_cell) - (1.0 / 12.0) * (values[:, :, :-3] + values[:, :, 3:])
    edges = jnp.clip(edges, jnp.minimum(left_cell, right_cell), jnp.maximum(left_cell, right_cell))
    centre = values[:, :, 2:width + 4]
    lower = edges[:, :, :width + 2]
    upper = edges[:, :, 1:width + 3]
    level = (upper - centre) * (centre - lower) <= 0.0
    lower = jnp.where(level, centre, lower)
    upper = jnp.where(level, centre, upper)
    spread = upper - lower
    tilt = spread * (centre - 0.5 * (lower + upper))
    bound = spread * spread / 6.0
    new_lower = jnp.where(tilt > bound, 3.0 * centre - 2.0 * upper, lower)
    new_upper = jnp.where(tilt < -bound, 3.0 * centre - 2.0 * lower, upper)
    spread = new_upper - new_lower
    curve = 6.0 * (centre - 0.5 * (new_lower + new_upper))
    backward = -courant
    from_left = courant * (new_upper[:, :, :-1] - 0.5 * courant * (spread[:, :, :-1] - (1.0 - courant * (2.0 / 3.0)) * curve[:, :, :-1]))
    from_right = courant * (new_lower[:, :, 1:] + 0.5 * backward * (spread[:, :, 1:] + (1.0 - backward * (2.0 / 3.0)) * curve[:, :, 1:]))
    flux = jnp.where(courant > 0.0, from_left, from_right)
    return values[:, :, 3:width + 3] - (flux[:, :, 1:] - flux[:, :, :-1])


def sweep_blocks(joined, lower_ghost, upper_ghost, lower_id, upper_id):
    edge_low = jnp.broadcast_to(joined[:, :, :1], lower_ghost.shape)
    edge_high = jnp.broadcast_to(joined[:, :, -1:], upper_ghost.shape)
    lower = jnp.where((lower_id >= 0)[:, None, None, None], lower_ghost, edge_low)
    upper = jnp.where((upper_id >= 0)[:, None, None, None], upper_ghost, edge_high)
    extended = jnp.concatenate([lower, joined, upper], axis=2)
    fields_num = joined.shape[1] - 1
    width = joined.shape[2]
    return ppm_update(extended[:, :fields_num], extended[:, fields_num:, 3:width + 4])


def reference(fields, speeds, neighbours, block_order, tiles, tile_fill, tile_dest):
    values = fields
    for direction in range(3):
        joined = directional(values, speeds, direction)
        layers = face_layers(joined)

        def one_block(item, direction=direction, layers=layers):
            single, links = item
            lower_id = links[2 * direction]
            upper_id = links[2 * direction + 1]
            lower_ghost = layers[jnp.maximum(lower_id, 0), 1][None]
            upper_ghost = layers[jnp.maximum(upper_id, 0), 0][None]
            return sweep_blocks(single[None], lower_ghost, upper_ghost, lower_id[None], upper_id[None])[0]

        swept = lax.map(one_block, (joined, neighbours))
        values = restore(swept, direction)
    blocks_out = jnp.take(values, block_order, axis=0)

    devices = N_GX * N_GY
    records = jnp.arange(TR, dtype=jnp.int32)
    live_mask = records[None, :] < tile_fill[:, None]
    drifted = jnp.concatenate([tiles[:, 0:3] + DRIFT * tiles[:, 3:6], tiles[:, 3:]], axis=1)
    drifted = jnp.where(live_mask[:, None, :], drifted, 0.0)
    target = tile_dest[:, 0]
    source = jnp.arange(TILES, dtype=jnp.int32) // TILES_DEV
    onehot = (target.reshape(devices, TILES_DEV)[:, :, None] == jnp.arange(devices, dtype=jnp.int32)[None, None, :]).astype(jnp.int32)
    before = jnp.cumsum(onehot, axis=1) - onehot
    ranking = jnp.sum(before * onehot, axis=2).reshape(-1).astype(jnp.int32)
    slot_index = target * (devices * CAPT) + source * CAPT + ranking
    tiles_out = jnp.zeros((devices * devices * CAPT, NA, TR), tiles.dtype).at[slot_index].set(drifted)
    fill_out = jnp.zeros((devices * devices * CAPT,), jnp.int32).at[slot_index].set(tile_fill)
    return blocks_out, tiles_out, fill_out
```

```python
import functools

import jax
import jax.numpy as jnp
from jax import lax
from jax.experimental import pallas as pl
from jax.experimental.pallas import tpu as pltpu
from jax.sharding import PartitionSpec as P

MESH = pl.DeviceIdType.MESH
NF = 6
NB = 2
CAPT = 2
DRIFT = 0.5
AXES = ("gx", "gy")


def pack_kernel(inverse, fills, tiles, out):
    lane = lax.broadcasted_iota(jnp.int32, (3, 128), 1)
    lane5 = lax.broadcasted_iota(jnp.int32, (5, 128), 1)

    def step(slot, carry):
        tile = inverse[slot]
        fill = fills[slot]
        head = tiles[tile, 0:3] + DRIFT * tiles[tile, 3:6]
        out[slot, 0:3] = jnp.where(lane < fill, head, 0.0)
        out[slot, 3:8] = jnp.where(lane5 < fill, tiles[tile, 3:8], 0.0)
        return carry

    lax.fori_loop(0, out.shape[0], step, 0, unroll=8)


def pack_tiles(tiles, inverse, fills, slots):
    return pl.pallas_call(
        pack_kernel,
        out_shape=jax.ShapeDtypeStruct((slots,) + tiles.shape[1:], tiles.dtype),
        in_specs=[
            pl.BlockSpec(memory_space=pltpu.SMEM),
            pl.BlockSpec(memory_space=pltpu.SMEM),
            pl.BlockSpec(memory_space=pltpu.VMEM),
        ],
        out_specs=pl.BlockSpec(memory_space=pltpu.VMEM),
        name="pack_tiles",
    )(inverse, fills, tiles)


def first_two(match, fill):
    width = match.shape[1]
    index = lax.broadcasted_iota(jnp.int32, match.shape, 1)
    first = jnp.min(jnp.where(match, index, width), axis=1)
    last = jnp.max(jnp.where(match, index, -1), axis=1)
    first_fill = jnp.sum(jnp.where(index == first[:, None], fill, 0), axis=1)
    second = jnp.where(last > first, last, width)
    second_fill = jnp.sum(jnp.where(index == second[:, None], fill, 0), axis=1)
    where = jnp.stack([first, second], axis=1).reshape(-1)
    return jnp.minimum(where, width - 1), jnp.stack([first_fill, second_fill], axis=1).reshape(-1)


def ppm(cells, courant):
    delta = [cells[i + 1] - cells[i] for i in range(9)]
    right, left = {}, {}
    for i in range(1, 8):
        step = 0.5 * delta[i] + (1.0 / 12.0) * (delta[i - 1] - delta[i + 1])
        step = jnp.minimum(
            jnp.maximum(step, jnp.minimum(delta[i], 0.0)), jnp.maximum(delta[i], 0.0)
        )
        right[i], left[i + 1] = step, delta[i] - step
    up, down = {}, {}
    for i in range(2, 8):
        r, l = right[i], left[i]
        r2, l2 = r + r, l + l
        up[i] = jnp.maximum(jnp.minimum(r, l2), 0.0) + jnp.minimum(jnp.maximum(r, l2), 0.0)
        down[i] = jnp.maximum(jnp.minimum(l, r2), 0.0) + jnp.minimum(jnp.maximum(l, r2), 0.0)
    flux = []
    for f in range(5):
        c, ca, cb = courant[f]
        a, b = f + 2, f + 3
        wind = c > 0.0
        flux.append(
            c * jnp.where(wind, cells[a], cells[b])
            + ca * jnp.where(wind, up[a], down[b])
            + cb * jnp.where(wind, down[a], up[b])
        )
    return [cells[r + 3] - (flux[r + 1] - flux[r]) for r in range(4)]


def coefficients(c):
    size = jnp.abs(c)
    rest = 1.0 - size
    side = size * rest
    return c, side * rest, side * size


def chosen(flag, shape, ghost, edge):
    return jnp.where(jnp.full(shape, flag, jnp.int32) != 0, ghost, edge)


def advance_kernel(devices, row, sel, fields, speeds, out, *scratch):
    (F, S, T, ST, O, SP0, SP1, SP2, C0, C1, C2), rest = scratch[:11], scratch[11:]
    pools = [rest[6 * s : 6 * s + 6] for s in range(3)]
    R = rest[18:24]
    (in_sem, face_send, face_recv, sp_send, sp_recv, mv_send, mv_recv, out_sem) = rest[24:]

    me = lax.axis_index("gx") * row + lax.axis_index("gy")
    core = lax.rem(me, 2)

    def device(d):
        d = lax.rem(d + devices, devices)
        return (d // row, lax.rem(d, row))

    peer = device(me + 1 - 2 * core)

    loads = [
        pltpu.make_async_copy(
            fields.at[:, :, :, pl.ds(q * 128, 128)], F.at[:, :, pl.ds(q * 32, 32), :], in_sem.at[q]
        )
        for q in range(8)
    ] + [
        pltpu.make_async_copy(
            speeds.at[:, :, :, pl.ds(q * 128, 128)],
            S.at[:, :, pl.ds(q * 32, 32), :],
            in_sem.at[8 + q],
        )
        for q in range(8)
    ]
    for load in loads:
        load.start()

    barrier = pltpu.get_barrier_semaphore()
    for offset in (-2, -1, 1, 2):
        pl.semaphore_signal(barrier, inc=1, device_id=device(me + offset), device_id_type=MESH)
    pl.semaphore_wait(barrier, 4)

    def remote(src, dst, send, recv, target):
        return pltpu.make_async_remote_copy(
            src_ref=src, dst_ref=dst, send_sem=send, recv_sem=recv,
            device_id=target, device_id_type=MESH,
        )

    class Exchange:
        def __init__(self, slot_at, send, recv):
            self.at, self.send, self.recv = slot_at, send, recv

        def start(self):
            own = self.at(2)
            self.far_up = remote(own, self.at(0), self.send.at[0], self.recv.at[0], device(me + 2))
            self.far_down = remote(
                own, self.at(4), self.send.at[1], self.recv.at[4], device(me - 2)
            )
            near = 1 + 2 * core
            self.near = remote(own, self.at(near), self.send.at[2], self.recv.at[near], peer)
            self.far_up.start()
            self.far_down.start()
            self.near.start()

        def forward(self):
            self.got(0)
            self.got(4)
            source, target = 4 - 4 * core, 3 - 2 * core
            self.passed = remote(
                self.at(source), self.at(target), self.send.at[3], self.recv.at[target], peer
            )
            self.passed.start()

        def got(self, slot):
            remote(
                self.at(slot), self.at(slot), self.send.at[0], self.recv.at[slot], peer
            ).wait_recv()

        def finish(self):
            self.got(1)
            self.got(3)

        def sent(self):
            for copy in (self.far_up, self.far_down, self.near, self.passed):
                copy.wait_send()

    def pairs(pool):
        return lambda slot: pool.at[pl.ds(2 * slot, 2)]

    def single(pool):
        return lambda slot: pool.at[slot]

    faces = [
        [
            Exchange(
                single(pools[s][f]) if s == 1 else pairs(pools[s][f]),
                face_send.at[s, f],
                face_recv.at[s, f],
            )
            for f in range(NF)
        ]
        for s in range(3)
    ]
    winds = [
        Exchange(at, sp_send.at[s], sp_recv.at[s])
        for s, at in enumerate((pairs(SP0), single(SP1), pairs(SP2)))
    ]

    sub = lax.broadcasted_iota(jnp.int32, (8, 128), 0)
    lane = lax.broadcasted_iota(jnp.int32, (8, 128), 1)

    def spot(b, d, h):
        return sel[b * 6 + 2 * d + h]

    def linked(b, d, h):
        return sel[12 + b * 6 + 2 * d + h]

    def pack_rows(s, f, A):
        pool = pools[s][f]
        for b in range(NB):
            for m in range(3):
                pool[4 + b, m] = A[b, f, pl.ds(m, 8, stride=32), :]
                pool[4 + b, 3 + m] = A[b, f, pl.ds(29 + m, 8, stride=32), :]

    def shift_up(x, ghost):
        return jnp.where(sub == 7, ghost, pltpu.roll(x, 7, 0))

    def shift_down(x, ghost):
        return jnp.where(sub == 0, ghost, pltpu.roll(x, 1, 0))

    def coef_rows(A, index, SP, d, C):
        def step(it, carry):
            b, c = it // 8, lax.rem(it, 8)
            base = c * 32
            own = [A[b, index, pl.ds(base + r, 8, stride=4), :] for r in range(4)]
            edge = A[b, index, pl.ds(base + 31, 1), :]
            ghost = SP[spot(b, d, 1), pl.ds(c, 1), :]
            ghost = chosen(linked(b, d, 1), (1, 128), ghost, edge)
            for r, value in enumerate(own + [shift_up(own[0], ghost)]):
                for n, part in enumerate(coefficients(value)):
                    C[it, 3 * r + n] = part
            return carry

        lax.fori_loop(0, 16, step, 0)

    def sweep_rows(s, f, A, C, strided):
        pool = pools[s][f]

        def step(it, carry):
            b, c = it // 8, lax.rem(it, 8)
            base = pl.multiple_of(c * 32, 32)
            own = [A[b, f, pl.ds(base + r, 8, stride=4), :] for r in range(4)]
            low_edge = A[b, f, pl.ds(base, 1), :]
            high_edge = A[b, f, pl.ds(base + 31, 1), :]
            low, high = spot(b, s, 0), spot(b, s, 1)
            low_on, high_on = linked(b, s, 0), linked(b, s, 1)
            before, after = [], []
            for m in range(3):
                ghost = chosen(low_on, (1, 128), pool[low, 3 + m, pl.ds(c, 1), :], low_edge)
                before.append(shift_down(own[m + 1], ghost))
                ghost = chosen(high_on, (1, 128), pool[high, m, pl.ds(c, 1), :], high_edge)
                after.append(shift_up(own[m], ghost))
            courant = [[C[it, 3 * r + n] for n in range(3)] for r in range(5)]
            result = ppm(before + own + after, courant)
            for r in range(4):
                if strided:
                    A[b, f, pl.ds(base + r, 8, stride=4), :] = result[r]
                else:
                    A[b, f, pl.ds(base + 8 * r, 8), :] = result[r]
            return carry

        lax.fori_loop(0, 16, step, 0)

    def side_up(x, ghost):
        return [
            pltpu.roll(jnp.where(lane < 32, x[1], x[0]), 96, 1),
            pltpu.roll(jnp.where(lane < 32, ghost, x[1]), 96, 1),
        ]

    def side_down(x, ghost):
        return [
            pltpu.roll(jnp.where(lane >= 96, ghost, x[0]), 32, 1),
            pltpu.roll(jnp.where(lane >= 96, x[0], x[1]), 32, 1),
        ]

    def pack_side(f):
        pool = pools[1][f]

        def step(o, carry):
            at = pl.multiple_of(o * 8, 8)
            for m in range(3):
                low = [T[b, f, pl.ds(m * 32 + at, 8), :] for b in range(NB)]
                high = [T[b, f, pl.ds(128 + (m + 1) * 32 + at, 8), :] for b in range(NB)]
                pool[2, m, pl.ds(at, 8), :] = jnp.where(
                    lane < 64,
                    jnp.where(lane < 32, low[0], pltpu.roll(low[1], 32, 1)),
                    jnp.where(lane >= 96, high[0], pltpu.roll(high[1], 96, 1)),
                )
            return carry

        lax.fori_loop(0, 4, step, 0)

    def coef_side():
        def step(it, carry):
            b, o = it // 4, lax.rem(it, 4)
            at = pl.multiple_of(o * 8, 8)
            own = [
                [ST[b, 0, pl.ds(h * 128 + g * 32 + at, 8), :] for h in range(2)] for g in range(4)
            ]
            where = spot(b, 1, 1)
            ghost = SP1[where // 2, pl.ds(at, 8), :]
            ghost = chosen(lax.rem(where, 2), (8, 128), pltpu.roll(ghost, 96, 1), ghost)
            ghost = chosen(linked(b, 1, 1), (8, 128), ghost, pltpu.roll(own[3][1], 32, 1))
            for r, value in enumerate(own + [side_up(own[0], ghost)]):
                for h in range(2):
                    for n, part in enumerate(coefficients(value[h])):
                        C1[it * 2 + h, 3 * r + n] = part
            return carry

        lax.fori_loop(0, 8, step, 0)

    def sweep_side(f):
        pool = pools[1][f]

        def step(it, carry):
            b, o = it // 4, lax.rem(it, 4)
            at = pl.multiple_of(o * 8, 8)
            own = [
                [T[b, f, pl.ds(h * 128 + g * 32 + at, 8), :] for h in range(2)] for g in range(4)
            ]
            low_edge = pltpu.roll(own[0][0], 96, 1)
            high_edge = pltpu.roll(own[3][1], 32, 1)
            low, high = spot(b, 1, 0), spot(b, 1, 1)
            low_on, high_on = linked(b, 1, 0), linked(b, 1, 1)
            before, after = [], []
            for m in range(3):
                ghost = pool[low // 2, m, pl.ds(at, 8), :]
                ghost = chosen(lax.rem(low, 2), (8, 128), pltpu.roll(ghost, 32, 1), ghost)
                ghost = chosen(low_on, (8, 128), ghost, low_edge)
                before.append(side_down(own[m + 1], ghost))
                ghost = pool[high // 2, m, pl.ds(at, 8), :]
                ghost = chosen(lax.rem(high, 2), (8, 128), pltpu.roll(ghost, 96, 1), ghost)
                ghost = chosen(high_on, (8, 128), ghost, high_edge)
                after.append(side_up(own[m], ghost))
            cells = before + own + after
            for h in range(2):
                courant = [[C1[it * 2 + h, 3 * r + n] for n in range(3)] for r in range(5)]
                result = ppm([x[h] for x in cells], courant)
                for g in range(4):
                    T[b, f, pl.ds(h * 128 + g * 32 + at, 8), :] = result[g]
            return carry

        lax.fori_loop(0, 8, step, 0)

    def turn(f):
        def step(it, carry):
            b, at = it // 2, pl.multiple_of(lax.rem(it, 2) * 128, 128)
            T[b, f, pl.ds(at, 128), :] = F[b, f, pl.ds(at, 128), :].T
            return carry

        lax.fori_loop(0, 4, step, 0)

    def turn_speeds():
        for n in range(2):
            def step(it, carry):
                b, h = it // 2, lax.rem(it, 2)
                rows = [
                    S[b, n + 1, pl.ds(h * 128 + q * 32 + r, 8, stride=4), :]
                    for q in range(4)
                    for r in range(4)
                ]
                at = pl.multiple_of(h * 128, 128)
                ST[b, n, pl.ds(at, 128), :] = jnp.concatenate(rows, axis=0).T
                return carry

            lax.fori_loop(0, 4, step, 0)

    def turn_back(f):
        def step(it, carry):
            b, h = it // 2, lax.rem(it, 2)
            back = T[b, f, pl.ds(pl.multiple_of(h * 128, 128), 128), :].T
            for q in range(4):
                for r in range(4):
                    R[f][2 + b, pl.ds(h * 128 + q * 32 + r, 8, stride=4), :] = back[
                        q * 32 + r * 8 : q * 32 + r * 8 + 8
                    ]
            return carry

        lax.fori_loop(0, 4, step, 0)

    for load in loads:
        load.wait()
    for b in range(NB):
        SP0[4 + b] = S[b, 0, pl.ds(0, 8, stride=32), :]
    winds[0].start()
    for f in range(NF):
        pack_rows(0, f, F)
        faces[0][f].start()
    turn_speeds()
    for b in range(NB):
        SP2[4 + b] = ST[b, 1, pl.ds(0, 8, stride=32), :]
    for o in range(4):
        at = o * 8
        SP1[2, pl.ds(at, 8), :] = jnp.where(
            lane < 32,
            ST[0, 0, pl.ds(at, 8), :],
            pltpu.roll(ST[1, 0, pl.ds(at, 8), :], 32, 1),
        )
    winds[1].start()
    winds[2].start()
    winds[0].forward()
    faces[0][0].forward()
    winds[0].finish()
    coef_rows(S, 0, SP0, 0, C0)

    moves = []
    for t in range(3 * NF):
        s, f = t // NF, t % NF
        if t + 1 < 3 * NF:
            faces[(t + 1) // NF][(t + 1) % NF].forward()
        if t == 1:
            winds[1].forward()
            winds[2].forward()
        if t == 4:
            winds[1].finish()
            winds[2].finish()
            coef_side()
            coef_rows(ST, 1, SP2, 2, C2)
        faces[s][f].finish()
        if s == 0:
            sweep_rows(0, f, F, C0, False)
            turn(f)
            pack_side(f)
            faces[1][f].start()
        elif s == 1:
            sweep_side(f)
            pack_rows(2, f, T)
            faces[2][f].start()
        else:
            sweep_rows(2, f, T, C2, True)
            turn_back(f)
            own = R[f].at[pl.ds(2, 2)]
            pair = [
                remote(own, R[f].at[pl.ds(0, 2)], mv_send.at[f, 0], mv_recv.at[f, 0], device(me + 1)),
                remote(own, R[f].at[pl.ds(4, 2)], mv_send.at[f, 1], mv_recv.at[f, 1], device(me - 1)),
            ]
            for copy in pair:
                copy.start()
            moves.append(pair)

    stores = []
    for f in range(NF):
        for copy in moves[f]:
            copy.wait_recv()
        for j in range(NB):
            def step(i, carry):
                at = pl.multiple_of(i * 8, 8)
                for q in range(8):
                    O[j, f, pl.ds(at, 8), pl.ds(q * 128, 128)] = R[f][
                        sel[24 + j], pl.ds(q * 32 + at, 8), :
                    ]
                return carry

            lax.fori_loop(0, 4, step, 0)
        stores.append(pltpu.make_async_copy(O.at[:, f], out.at[:, f], out_sem.at[f]))
        stores[-1].start()
    for group in faces + [winds]:
        for exchange in group:
            exchange.sent()
    for pair in moves:
        for copy in pair:
            copy.wait_send()
    for store in stores:
        store.wait()


def advance(fields, speeds, sel, devices, row):
    f32 = jnp.float32
    dma = pltpu.SemaphoreType.DMA
    scratch = [
        pltpu.VMEM((NB, NF, 256, 128), f32),
        pltpu.VMEM((NB, 3, 256, 128), f32),
        pltpu.VMEM((NB, NF, 256, 128), f32),
        pltpu.VMEM((NB, 2, 256, 128), f32),
        pltpu.VMEM((NB, NF, 32, 1024), f32),
        pltpu.VMEM((10, 8, 128), f32),
        pltpu.VMEM((5, 32, 128), f32),
        pltpu.VMEM((10, 8, 128), f32),
    ]
    scratch += [pltpu.VMEM((16, 15, 8, 128), f32) for _ in range(3)]
    for s in range(3):
        shape = (5, 3, 32, 128) if s == 1 else (10, 6, 8, 128)
        scratch += [pltpu.VMEM(shape, f32) for _ in range(NF)]
    scratch += [pltpu.VMEM((6, 256, 128), f32) for _ in range(NF)]
    scratch += [
        dma((16,)), dma((3, NF, 4)), dma((3, NF, 5)), dma((3, 4)), dma((3, 5)),
        dma((NF, 2)), dma((NF, 2)), dma((NF,)),
    ]
    return pl.pallas_call(
        functools.partial(advance_kernel, devices, row),
        out_shape=jax.ShapeDtypeStruct(fields.shape, f32),
        in_specs=[
            pl.BlockSpec(memory_space=pltpu.SMEM),
            pl.BlockSpec(memory_space=pl.ANY),
            pl.BlockSpec(memory_space=pl.ANY),
        ],
        out_specs=pl.BlockSpec(memory_space=pl.ANY),
        scratch_shapes=scratch,
        name="advance_blocks",
        compiler_params=pltpu.CompilerParams(
            collective_id=0, has_side_effects=True, vmem_limit_bytes=40 * 1024 * 1024
        ),
    )(sel, fields, speeds)


def body(fields, speeds, neighbours, block_order, tiles, tile_fill, tile_dest):
    row = lax.axis_size("gy")
    devices = lax.axis_size(AXES)
    me = lax.axis_index(AXES)
    first_block = me * NB

    target = tile_dest[:, 0]
    meta = jnp.stack([target, tile_fill])
    everyone = lax.all_gather(meta, AXES)

    links = lax.dynamic_slice_in_dim(neighbours, first_block, NB).reshape(-1)
    spots = jnp.clip((links // 2 - me + 2) * 2 + links % 2, 0, 9)
    incoming = lax.dynamic_slice_in_dim(block_order, first_block, NB)
    picks = jnp.clip((incoming // 2 - me + 1) * 2 + incoming % 2, 0, 5)
    sel = jnp.concatenate([spots, (links >= 0).astype(jnp.int32), picks])

    match = target[None, :] == jnp.arange(devices, dtype=jnp.int32)[:, None]
    inverse, fills = first_two(match, tile_fill[None, :])
    outgoing = pack_tiles(tiles, inverse, fills, devices * CAPT)
    tiles_out = lax.all_to_all(outgoing, AXES, split_axis=0, concat_axis=0, tiled=True)

    blocks_out = advance(fields, speeds, sel, devices, row)
    _, fill_out = first_two(everyone[:, 0] == me, everyone[:, 1])
    return blocks_out, tiles_out, fill_out


def solution(mesh):
    blocks = P(AXES, None, None, None)
    return jax.shard_map(
        body,
        mesh=mesh,
        in_specs=(blocks, blocks, P(), P(), P(AXES, None, None), P(AXES), P(AXES, None)),
        out_specs=(blocks, P(AXES, None, None), P(AXES)),
        check_vma=False,
    )
```

```python
import functools

import jax
import jax.numpy as jnp
from jax import lax
from jax.experimental import pallas as pl
from jax.experimental.pallas import tpu as pltpu
from jax.sharding import PartitionSpec as P

MESH = pl.DeviceIdType.MESH
NF = 6
NB = 2
CAPT = 2
DRIFT = 0.5
AXES = ("gx", "gy")


def ppm(cells, courant):
    delta = [cells[i + 1] - cells[i] for i in range(9)]
    right, left = {}, {}
    for i in range(1, 8):
        step = 0.5 * delta[i] + (1.0 / 12.0) * (delta[i - 1] - delta[i + 1])
        step = jnp.minimum(
            jnp.maximum(step, jnp.minimum(delta[i], 0.0)), jnp.maximum(delta[i], 0.0)
        )
        right[i], left[i + 1] = step, delta[i] - step
    up, down = {}, {}
    for i in range(2, 8):
        r, l = right[i], left[i]
        r2, l2 = r + r, l + l
        up[i] = jnp.maximum(jnp.minimum(r, l2), 0.0) + jnp.minimum(jnp.maximum(r, l2), 0.0)
        down[i] = jnp.maximum(jnp.minimum(l, r2), 0.0) + jnp.minimum(jnp.maximum(l, r2), 0.0)
    flux = []
    for f in range(5):
        c, ca, cb = courant[f]
        a, b = f + 2, f + 3
        wind = c > 0.0
        flux.append(
            c * jnp.where(wind, cells[a], cells[b])
            + ca * jnp.where(wind, up[a], down[b])
            + cb * jnp.where(wind, down[a], up[b])
        )
    return [cells[r + 3] - (flux[r + 1] - flux[r]) for r in range(4)]


def coefficients(c):
    size = jnp.abs(c)
    rest = 1.0 - size
    side = size * rest
    return c, side * rest, side * size


def chosen(flag, shape, ghost, edge):
    return jnp.where(jnp.full(shape, flag, jnp.int32) != 0, ghost, edge)


def tree(op, x):
    parts = [x[8 * i : 8 * i + 8] for i in range(16)]
    while len(parts) > 1:
        parts = [op(p, q) for p, q in zip(parts[::2], parts[1::2])]
    value = parts[0]
    for shift in (4, 2, 1):
        value = op(value, pltpu.roll(value, shift, 0))
    return value


FILL_AT = (3, 5, 7, 9)
RING_AT = 4
LAST_AT = (8, 10)
ORDER = sorted(((s, f) for s in range(3) for f in range(NF)), key=lambda t: (2 * t[1] + 6 * t[0], -t[0]))


def advance_kernel(devices, row, sel, fields, speeds, tiles, dest, fill, *refs):
    out, tiles_out, fill_out = refs[:3]
    (F, S, T, ST, O, SP0, SP1, SP2, C0, C1, C2), rest = refs[3:14], refs[14:]
    pools = [rest[6 * s : 6 * s + 6] for s in range(3)]
    R, rest = rest[18:24], rest[24:]
    (TL, G, INV, INVS), B0, B1, B2, rest = rest[:4], rest[4:6], rest[6:8], rest[8:10], rest[10:]
    (in_sem, face_send, face_recv, sp_send, sp_recv, mv_send, mv_recv, out_sem) = rest[:8]
    (inv_sem, ring_send, ring_recv, own_sem, last_send, last_recv, all_send, all_recv) = rest[8:]

    gx, gy = lax.axis_index("gx"), lax.axis_index("gy")
    me = gx * row + gy
    core = lax.rem(gy, 2)
    gz, yc, y = gy // 8, lax.rem(gy, 8), lax.rem(gy // 2, 4)

    def along_x(k):
        x = lax.rem(gx + k, 4)
        return x, (x, gy)

    def along_z(k):
        z = lax.rem(gz + k, 4)
        return z, (gx, z * 8 + yc)

    def along_yc(k):
        n = lax.rem(yc + k, 8)
        return n, (gx, gz * 8 + n)

    def along_y(k):
        n = lax.rem(y + k, 4)
        return n, (gx, gz * 8 + n * 2 + core)

    def device(d):
        d = lax.rem(d + devices, devices)
        return (d // row, lax.rem(d, row))

    peer = device(me + 1 - 2 * core)

    loads = [
        pltpu.make_async_copy(
            fields.at[:, :, :, pl.ds(q * 128, 128)], F.at[:, :, pl.ds(q * 32, 32), :], in_sem.at[q]
        )
        for q in range(8)
    ] + [
        pltpu.make_async_copy(
            speeds.at[:, :, :, pl.ds(q * 128, 128)],
            S.at[:, :, pl.ds(q * 32, 32), :],
            in_sem.at[8 + q],
        )
        for q in range(8)
    ]
    tile_load = pltpu.make_async_copy(tiles, TL, in_sem.at[16])
    for load in loads + [tile_load]:
        load.start()

    barrier = pltpu.get_barrier_semaphore()
    greeted = [device(me + offset) for offset in (-2, -1, 1, 2)]
    greeted += [along_x(k)[1] for k in (1, 2, 3)] + [along_z(k)[1] for k in (1, 2, 3)]
    greeted += [along_yc(k)[1] for k in range(1, 8)]
    for other in greeted:
        pl.semaphore_signal(barrier, inc=1, device_id=other, device_id_type=MESH)
    pl.semaphore_wait(barrier, len(greeted))

    def remote(src, dst, send, recv, target):
        return pltpu.make_async_remote_copy(
            src_ref=src, dst_ref=dst, send_sem=send, recv_sem=recv,
            device_id=target, device_id_type=MESH,
        )

    class Exchange:
        def __init__(self, slot_at, send, recv):
            self.at, self.send, self.recv = slot_at, send, recv

        def start(self):
            own = self.at(2)
            self.far_up = remote(own, self.at(0), self.send.at[0], self.recv.at[0], device(me + 2))
            self.far_down = remote(
                own, self.at(4), self.send.at[1], self.recv.at[4], device(me - 2)
            )
            near = 1 + 2 * core
            self.near = remote(own, self.at(near), self.send.at[2], self.recv.at[near], peer)
            self.far_up.start()
            self.far_down.start()
            self.near.start()

        def forward(self):
            self.got(0)
            self.got(4)
            source, target = 4 - 4 * core, 3 - 2 * core
            self.passed = remote(
                self.at(source), self.at(target), self.send.at[3], self.recv.at[target], peer
            )
            self.passed.start()

        def got(self, slot):
            remote(
                self.at(slot), self.at(slot), self.send.at[0], self.recv.at[slot], peer
            ).wait_recv()

        def finish(self):
            self.got(1)
            self.got(3)

        def sent(self):
            for copy in (self.far_up, self.far_down, self.near, self.passed):
                copy.wait_send()

    def pairs(pool):
        return lambda slot: pool.at[pl.ds(2 * slot, 2)]

    def single(pool):
        return lambda slot: pool.at[slot]

    faces = [
        [
            Exchange(
                single(pools[s][f]) if s == 1 else pairs(pools[s][f]),
                face_send.at[s, f],
                face_recv.at[s, f],
            )
            for f in range(NF)
        ]
        for s in range(3)
    ]
    winds = [
        Exchange(at, sp_send.at[s], sp_recv.at[s])
        for s, at in enumerate((pairs(SP0), single(SP1), pairs(SP2)))
    ]

    sub = lax.broadcasted_iota(jnp.int32, (8, 128), 0)
    lane = lax.broadcasted_iota(jnp.int32, (8, 128), 1)

    def spot(b, d, h):
        return sel[b * 6 + 2 * d + h]

    def linked(b, d, h):
        return sel[12 + b * 6 + 2 * d + h]

    def pack_rows(s, f, A):
        pool = pools[s][f]
        for b in range(NB):
            for m in range(3):
                pool[4 + b, m] = A[b, f, pl.ds(m, 8, stride=32), :]
                pool[4 + b, 3 + m] = A[b, f, pl.ds(29 + m, 8, stride=32), :]

    def shift_up(x, ghost):
        return jnp.where(sub == 7, ghost, pltpu.roll(x, 7, 0))

    def shift_down(x, ghost):
        return jnp.where(sub == 0, ghost, pltpu.roll(x, 1, 0))

    def coef_rows(A, index, SP, d, C):
        def step(it, carry):
            b, c = it // 8, lax.rem(it, 8)
            base = c * 32
            own = [A[b, index, pl.ds(base + r, 8, stride=4), :] for r in range(4)]
            edge = A[b, index, pl.ds(base + 31, 1), :]
            ghost = SP[spot(b, d, 1), pl.ds(c, 1), :]
            ghost = chosen(linked(b, d, 1), (1, 128), ghost, edge)
            for r, value in enumerate(own + [shift_up(own[0], ghost)]):
                for n, part in enumerate(coefficients(value)):
                    C[it, 3 * r + n] = part
            return carry

        lax.fori_loop(0, 16, step, 0)

    def sweep_rows(s, f, A, C, strided):
        pool = pools[s][f]

        def step(it, carry):
            b, c = it // 8, lax.rem(it, 8)
            base = pl.multiple_of(c * 32, 32)
            own = [A[b, f, pl.ds(base + r, 8, stride=4), :] for r in range(4)]
            low_edge = A[b, f, pl.ds(base, 1), :]
            high_edge = A[b, f, pl.ds(base + 31, 1), :]
            low, high = spot(b, s, 0), spot(b, s, 1)
            low_on, high_on = linked(b, s, 0), linked(b, s, 1)
            before, after = [], []
            for m in range(3):
                ghost = chosen(low_on, (1, 128), pool[low, 3 + m, pl.ds(c, 1), :], low_edge)
                before.append(shift_down(own[m + 1], ghost))
                ghost = chosen(high_on, (1, 128), pool[high, m, pl.ds(c, 1), :], high_edge)
                after.append(shift_up(own[m], ghost))
            courant = [[C[it, 3 * r + n] for n in range(3)] for r in range(5)]
            result = ppm(before + own + after, courant)
            for r in range(4):
                if strided:
                    A[b, f, pl.ds(base + r, 8, stride=4), :] = result[r]
                else:
                    A[b, f, pl.ds(base + 8 * r, 8), :] = result[r]
            return carry

        lax.fori_loop(0, 16, step, 0, unroll=4)

    def side_up(x, ghost):
        return [
            pltpu.roll(jnp.where(lane < 32, x[1], x[0]), 96, 1),
            pltpu.roll(jnp.where(lane < 32, ghost, x[1]), 96, 1),
        ]

    def side_down(x, ghost):
        return [
            pltpu.roll(jnp.where(lane >= 96, ghost, x[0]), 32, 1),
            pltpu.roll(jnp.where(lane >= 96, x[0], x[1]), 32, 1),
        ]

    def pack_side(f):
        pool = pools[1][f]

        def step(o, carry):
            at = pl.multiple_of(o * 8, 8)
            for m in range(3):
                low = [T[b, f, pl.ds(m * 32 + at, 8), :] for b in range(NB)]
                high = [T[b, f, pl.ds(128 + (m + 1) * 32 + at, 8), :] for b in range(NB)]
                pool[2, m, pl.ds(at, 8), :] = jnp.where(
                    lane < 64,
                    jnp.where(lane < 32, low[0], pltpu.roll(low[1], 32, 1)),
                    jnp.where(lane >= 96, high[0], pltpu.roll(high[1], 96, 1)),
                )
            return carry

        lax.fori_loop(0, 4, step, 0)

    def coef_side():
        def step(it, carry):
            b, o = it // 4, lax.rem(it, 4)
            at = pl.multiple_of(o * 8, 8)
            own = [
                [ST[b, 0, pl.ds(h * 128 + g * 32 + at, 8), :] for h in range(2)] for g in range(4)
            ]
            where = spot(b, 1, 1)
            ghost = SP1[where // 2, pl.ds(at, 8), :]
            ghost = chosen(lax.rem(where, 2), (8, 128), pltpu.roll(ghost, 96, 1), ghost)
            ghost = chosen(linked(b, 1, 1), (8, 128), ghost, pltpu.roll(own[3][1], 32, 1))
            for r, value in enumerate(own + [side_up(own[0], ghost)]):
                for h in range(2):
                    for n, part in enumerate(coefficients(value[h])):
                        C1[it * 2 + h, 3 * r + n] = part
            return carry

        lax.fori_loop(0, 8, step, 0)

    def sweep_side(f):
        pool = pools[1][f]

        def step(it, carry):
            b, o = it // 4, lax.rem(it, 4)
            at = pl.multiple_of(o * 8, 8)
            own = [
                [T[b, f, pl.ds(h * 128 + g * 32 + at, 8), :] for h in range(2)] for g in range(4)
            ]
            low_edge = pltpu.roll(own[0][0], 96, 1)
            high_edge = pltpu.roll(own[3][1], 32, 1)
            low, high = spot(b, 1, 0), spot(b, 1, 1)
            low_on, high_on = linked(b, 1, 0), linked(b, 1, 1)
            before, after = [], []
            for m in range(3):
                ghost = pool[low // 2, m, pl.ds(at, 8), :]
                ghost = chosen(lax.rem(low, 2), (8, 128), pltpu.roll(ghost, 32, 1), ghost)
                ghost = chosen(low_on, (8, 128), ghost, low_edge)
                before.append(side_down(own[m + 1], ghost))
                ghost = pool[high // 2, m, pl.ds(at, 8), :]
                ghost = chosen(lax.rem(high, 2), (8, 128), pltpu.roll(ghost, 96, 1), ghost)
                ghost = chosen(high_on, (8, 128), ghost, high_edge)
                after.append(side_up(own[m], ghost))
            cells = before + own + after
            for h in range(2):
                courant = [[C1[it * 2 + h, 3 * r + n] for n in range(3)] for r in range(5)]
                result = ppm([x[h] for x in cells], courant)
                for g in range(4):
                    T[b, f, pl.ds(h * 128 + g * 32 + at, 8), :] = result[g]
            return carry

        lax.fori_loop(0, 8, step, 0, unroll=2)

    def turn(f):
        def step(it, carry):
            b, at = it // 2, pl.multiple_of(lax.rem(it, 2) * 128, 128)
            T[b, f, pl.ds(at, 128), :] = F[b, f, pl.ds(at, 128), :].T
            return carry

        lax.fori_loop(0, 4, step, 0, unroll=4)

    def turn_speeds():
        for n in range(2):
            def step(it, carry):
                b, h = it // 2, lax.rem(it, 2)
                rows = [
                    S[b, n + 1, pl.ds(h * 128 + q * 32 + r, 8, stride=4), :]
                    for q in range(4)
                    for r in range(4)
                ]
                at = pl.multiple_of(h * 128, 128)
                ST[b, n, pl.ds(at, 128), :] = jnp.concatenate(rows, axis=0).T
                return carry

            lax.fori_loop(0, 4, step, 0)

    def turn_back(f):
        def step(it, carry):
            b, h = it // 2, lax.rem(it, 2)
            back = T[b, f, pl.ds(pl.multiple_of(h * 128, 128), 128), :].T
            for q in range(4):
                for r in range(4):
                    R[f][2 + b, pl.ds(h * 128 + q * 32 + r, 8, stride=4), :] = back[
                        q * 32 + r * 8 : q * 32 + r * 8 + 8
                    ]
            return carry

        lax.fori_loop(0, 4, step, 0, unroll=4)

    def find_tiles():
        t = lax.broadcasted_iota(jnp.int32, (128, 128), 0)
        p = lax.broadcasted_iota(jnp.int32, (128, 128), 1)
        dests = jnp.broadcast_to(dest[...], (128, 128)).T
        fills = jnp.broadcast_to(fill[...], (128, 128)).T
        match = dests == p

        def rows(x):
            return jnp.concatenate([x] * 16, axis=0)

        first = tree(jnp.minimum, jnp.where(match, t, 128))
        last = tree(jnp.maximum, jnp.where(match, t, -1))
        second = jnp.where(last > first, last, 128)
        first_fill = tree(jnp.add, jnp.where(t == rows(first), fills, 0))
        second_fill = tree(jnp.add, jnp.where(t == rows(second), fills, 0))
        where = jnp.where(sub == 0, jnp.minimum(first, 127), jnp.minimum(second, 127))
        INV[...] = jnp.where(sub < 2, where, jnp.where(sub == 2, first_fill, second_fill))
        G[me, 0:1] = first_fill[0:1]
        G[me, 1:2] = second_fill[0:1]
        copy = pltpu.make_async_copy(INV, INVS, inv_sem)
        copy.start()
        return copy

    def pack_tiles():
        def step(i, carry):
            for n in range(8):
                for h in range(CAPT):
                    x = TL[INVS[h, i * 8 + n]]
                    moved = jnp.where(sub < 3, x + DRIFT * pltpu.roll(x, 5, 0), x)
                    live = lane < jnp.full((8, 128), INVS[2 + h, i * 8 + n], jnp.int32)
                    B0[h][i // 4, lax.rem(i, 4), n] = jnp.where(live, moved, 0.0)
            return carry

        lax.fori_loop(0, 16, step, 0)

    def at_x(ref, n):
        return ref.at[n]

    def at_z(ref, n):
        return ref.at[:, n]

    class Ring:
        def __init__(self, h, turn):
            source, target = ((B0, B1), (B1, B2))[turn]
            x_now = h == turn
            along, at, here = (along_x, at_x, gx) if x_now else (along_z, at_z, gz)
            self.own = pltpu.make_async_copy(
                at(source[h], here), at(target[h], here), own_sem.at[h, turn]
            )
            self.copies, self.arrivals = [], []
            for k in (1, 2, 3):
                n, other = along(k)
                send, recv = ring_send.at[h, turn, k], ring_recv.at[h, turn, k]
                self.copies.append(
                    remote(at(source[h], n), at(target[h], here), send, recv, other)
                )
                n, other = along(4 - k)
                self.arrivals.append(
                    remote(at(source[h], n), at(target[h], n), send, recv, other)
                )

        def start(self):
            for copy in self.copies:
                copy.start()
            self.own.start()

        def finish(self):
            self.own.wait()
            for copy in self.arrivals:
                copy.wait_recv()

        def sent(self):
            for copy in self.copies:
                copy.wait_send()

    class Last:
        def __init__(self, h):
            self.own = pltpu.make_async_copy(
                B2[h].at[:, :, yc], tiles_out.at[:, :, yc, h], own_sem.at[h, 2]
            )
            self.copies, self.arrivals = [], []
            for k in range(1, 8):
                send, recv = last_send.at[h, k], last_recv.at[h, k]
                n, other = along_yc(k)
                self.copies.append(
                    remote(B2[h].at[:, :, n], tiles_out.at[:, :, yc, h], send, recv, other)
                )
                n, other = along_yc(8 - k)
                self.arrivals.append(
                    remote(B2[h].at[:, :, n], tiles_out.at[:, :, n, h], send, recv, other)
                )

        start, finish, sent = Ring.start, Ring.finish, Ring.sent

    class Fills:
        def __init__(self, n):
            size = (1, 2, 8, 32)[n]
            base = me // size * size
            mine = G.at[pl.ds(base, size)]
            self.copies, self.arrivals = [], []
            for k in (1,) if n == 0 else (1, 2, 3):
                send, recv = all_send.at[n, k], all_recv.at[n, k]
                for list_, j in ((self.copies, k), (self.arrivals, (2 if n == 0 else 4) - k)):
                    if n == 0:
                        other, start = peer, me + 1 - 2 * core
                    else:
                        at, other = (along_y, along_z, along_x)[n - 1](j)
                        start = base + (at - (y, gz, gx)[n - 1]) * size
                    where = mine if list_ is self.copies else G.at[pl.ds(start, size)]
                    list_.append(remote(mine, where, send, recv, other))

        def start(self):
            for copy in self.copies:
                copy.start()

        def finish(self):
            for copy in self.arrivals:
                copy.wait_recv()

        sent = Ring.sent

    rings = [[Ring(h, turn) for turn in range(2)] for h in range(CAPT)]
    lasts = [Last(h) for h in range(CAPT)]
    fill_steps = [Fills(n) for n in range(4)]

    def own_fills():
        flat = lax.broadcasted_iota(jnp.int32, (2, 128), 0) * 128
        flat = flat + lax.broadcasted_iota(jnp.int32, (2, 128), 1)
        mine = lax.broadcasted_iota(jnp.int32, (2, 128), 1) == me

        def step(i, total):
            for n in range(8):
                source = i * 8 + n
                value = jnp.sum(jnp.where(mine, G[source], 0), axis=1, keepdims=True)
                for h in range(CAPT):
                    total = jnp.where(
                        flat == source * CAPT + h,
                        jnp.broadcast_to(value[h : h + 1], (2, 128)),
                        total,
                    )
            return total

        fill_out[...] = lax.fori_loop(0, 16, step, jnp.zeros((2, 128), jnp.int32))

    for load in loads:
        load.wait()
    for b in range(NB):
        SP0[4 + b] = S[b, 0, pl.ds(0, 8, stride=32), :]
    winds[0].start()
    for f in range(NF):
        pack_rows(0, f, F)
        faces[0][f].start()
    found = find_tiles()
    fill_steps[0].start()
    turn_speeds()
    found.wait()
    tile_load.wait()
    pack_tiles()
    for h in range(CAPT):
        rings[h][0].start()
    for b in range(NB):
        SP2[4 + b] = ST[b, 1, pl.ds(0, 8, stride=32), :]
    for o in range(4):
        at = o * 8
        SP1[2, pl.ds(at, 8), :] = jnp.where(
            lane < 32,
            ST[0, 0, pl.ds(at, 8), :],
            pltpu.roll(ST[1, 0, pl.ds(at, 8), :], 32, 1),
        )
    winds[1].start()
    winds[2].start()
    winds[0].forward()
    faces[0][0].forward()
    winds[0].finish()
    coef_rows(S, 0, SP0, 0, C0)

    moves = {}
    first_of = {s: min(t for t in range(3 * NF) if ORDER[t][0] == s) for s in range(3)}
    for t in range(3 * NF):
        s, f = ORDER[t]
        if t + 1 < 3 * NF:
            after_s, after_f = ORDER[t + 1]
            faces[after_s][after_f].forward()
        if t == 1:
            winds[1].forward()
            winds[2].forward()
        if t == first_of[1]:
            winds[1].finish()
            coef_side()
        if t == first_of[2]:
            winds[2].finish()
            coef_rows(ST, 1, SP2, 2, C2)
        if t in FILL_AT:
            n = FILL_AT.index(t)
            fill_steps[n].finish()
            if n < 3:
                fill_steps[n + 1].start()
            else:
                own_fills()
        if t == RING_AT:
            for h in range(CAPT):
                rings[h][0].finish()
                rings[h][1].start()
        if t in LAST_AT:
            h = LAST_AT.index(t)
            rings[h][1].finish()
            lasts[h].start()
        faces[s][f].finish()
        if s == 0:
            sweep_rows(0, f, F, C0, False)
            turn(f)
            pack_side(f)
            faces[1][f].start()
        elif s == 1:
            sweep_side(f)
            pack_rows(2, f, T)
            faces[2][f].start()
        else:
            sweep_rows(2, f, T, C2, True)
            turn_back(f)
            own = R[f].at[pl.ds(2, 2)]
            pair = [
                remote(own, R[f].at[pl.ds(0, 2)], mv_send.at[f, 0], mv_recv.at[f, 0], device(me + 1)),
                remote(own, R[f].at[pl.ds(4, 2)], mv_send.at[f, 1], mv_recv.at[f, 1], device(me - 1)),
            ]
            for copy in pair:
                copy.start()
            moves[f] = pair

    stores = []
    for f in range(NF):
        for copy in moves[f]:
            copy.wait_recv()
        for j in range(NB):
            def step(i, carry):
                at = pl.multiple_of(i * 8, 8)
                for q in range(8):
                    O[j, f, pl.ds(at, 8), pl.ds(q * 128, 128)] = R[f][
                        sel[24 + j], pl.ds(q * 32 + at, 8), :
                    ]
                return carry

            lax.fori_loop(0, 4, step, 0)
        stores.append(pltpu.make_async_copy(O.at[:, f], out.at[:, f], out_sem.at[f]))
        stores[-1].start()
    for last in lasts:
        last.finish()
    for group in faces + [winds, fill_steps, lasts] + rings:
        for exchange in group:
            exchange.sent()
    for pair in moves.values():
        for copy in pair:
            copy.wait_send()
    for store in stores:
        store.wait()


def advance(fields, speeds, sel, tiles, dest, fill, devices, row):
    f32, i32 = jnp.float32, jnp.int32
    dma = pltpu.SemaphoreType.DMA
    scratch = [
        pltpu.VMEM((NB, NF, 256, 128), f32),
        pltpu.VMEM((NB, 3, 256, 128), f32),
        pltpu.VMEM((NB, NF, 256, 128), f32),
        pltpu.VMEM((NB, 2, 256, 128), f32),
        pltpu.VMEM((NB, NF, 32, 1024), f32),
        pltpu.VMEM((10, 8, 128), f32),
        pltpu.VMEM((5, 32, 128), f32),
        pltpu.VMEM((10, 8, 128), f32),
    ]
    scratch += [pltpu.VMEM((16, 15, 8, 128), f32) for _ in range(3)]
    for s in range(3):
        shape = (5, 3, 32, 128) if s == 1 else (10, 6, 8, 128)
        scratch += [pltpu.VMEM(shape, f32) for _ in range(NF)]
    scratch += [pltpu.VMEM((6, 256, 128), f32) for _ in range(NF)]
    scratch += [
        pltpu.VMEM((128, 8, 128), f32),
        pltpu.VMEM((128, CAPT, 128), i32),
        pltpu.VMEM((8, 128), i32),
        pltpu.SMEM((8, 128), i32),
    ]
    scratch += [pltpu.VMEM((4, 4, 8, 8, 128), f32) for _ in range(3 * CAPT)]
    scratch += [
        dma((17,)), dma((3, NF, 4)), dma((3, NF, 5)), dma((3, 4)), dma((3, 5)),
        dma((NF, 2)), dma((NF, 2)), dma((NF,)),
        dma(()), dma((CAPT, 2, 4)), dma((CAPT, 2, 4)), dma((CAPT, 3)),
        dma((CAPT, 8)), dma((CAPT, 8)), dma((4, 4)), dma((4, 4)),
    ]
    return pl.pallas_call(
        functools.partial(advance_kernel, devices, row),
        out_shape=(
            jax.ShapeDtypeStruct(fields.shape, f32),
            jax.ShapeDtypeStruct((4, 4, 8, CAPT, 8, 128), f32),
            jax.ShapeDtypeStruct((CAPT, 128), i32),
        ),
        in_specs=[
            pl.BlockSpec(memory_space=pltpu.SMEM),
            pl.BlockSpec(memory_space=pltpu.HBM),
            pl.BlockSpec(memory_space=pltpu.HBM),
            pl.BlockSpec(memory_space=pltpu.HBM),
            pl.BlockSpec(memory_space=pltpu.VMEM),
            pl.BlockSpec(memory_space=pltpu.VMEM),
        ],
        out_specs=(
            pl.BlockSpec(memory_space=pl.ANY),
            pl.BlockSpec(memory_space=pl.ANY),
            pl.BlockSpec(memory_space=pltpu.VMEM),
        ),
        scratch_shapes=scratch,
        name="advance_blocks",
        compiler_params=pltpu.CompilerParams(
            collective_id=0, has_side_effects=True, vmem_limit_bytes=40 * 1024 * 1024
        ),
    )(sel, fields, speeds, tiles, dest, fill)


def body(fields, speeds, neighbours, block_order, tiles, tile_fill, tile_dest):
    row = lax.axis_size("gy")
    devices = lax.axis_size(AXES)
    me = lax.axis_index(AXES)
    first_block = me * NB

    links = lax.dynamic_slice_in_dim(neighbours, first_block, NB).reshape(-1)
    spots = jnp.clip((links // 2 - me + 2) * 2 + links % 2, 0, 9)
    incoming = lax.dynamic_slice_in_dim(block_order, first_block, NB)
    picks = jnp.clip((incoming // 2 - me + 1) * 2 + incoming % 2, 0, 5)
    sel = jnp.concatenate([spots, (links >= 0).astype(jnp.int32), picks])

    blocks_out, tiles_out, fill_out = advance(
        fields, speeds, sel, tiles, tile_dest.reshape(1, -1), tile_fill.reshape(1, -1), devices, row
    )
    return blocks_out, tiles_out.reshape((-1,) + tiles.shape[1:]), fill_out.reshape(-1)


def solution(mesh):
    blocks = P(AXES, None, None, None)
    return jax.shard_map(
        body,
        mesh=mesh,
        in_specs=(blocks, blocks, P(), P(), P(AXES, None, None), P(AXES), P(AXES, None)),
        out_specs=(blocks, P(AXES, None, None), P(AXES)),
        check_vma=False,
    )
```

```python
import functools

import jax
import jax.numpy as jnp
from jax import lax
from jax.experimental import pallas as pl
from jax.experimental.pallas import tpu as pltpu
from jax.sharding import PartitionSpec as P

MESH = pl.DeviceIdType.MESH
NF = 6
NB = 2
CAPT = 2
DRIFT = 0.5
AXES = ("gx", "gy")


def ppm(cells, courant):
    n = len(cells) - 6
    delta = [cells[i + 1] - cells[i] for i in range(n + 5)]
    right, left = {}, {}
    for i in range(1, n + 4):
        step = 0.5 * delta[i] + (1.0 / 12.0) * (delta[i - 1] - delta[i + 1])
        step = jnp.minimum(
            jnp.maximum(step, jnp.minimum(delta[i], 0.0)), jnp.maximum(delta[i], 0.0)
        )
        right[i], left[i + 1] = step, delta[i] - step
    up, down = {}, {}
    for i in range(2, n + 4):
        r, l = right[i], left[i]
        r2, l2 = r + r, l + l
        up[i] = jnp.maximum(jnp.minimum(r, l2), 0.0) + jnp.minimum(jnp.maximum(r, l2), 0.0)
        down[i] = jnp.maximum(jnp.minimum(l, r2), 0.0) + jnp.minimum(jnp.maximum(l, r2), 0.0)
    flux = []
    for f in range(n + 1):
        c, ca, cb = courant[f]
        a, b = f + 2, f + 3
        wind = c > 0.0
        flux.append(
            c * jnp.where(wind, cells[a], cells[b])
            + ca * jnp.where(wind, up[a], down[b])
            + cb * jnp.where(wind, down[a], up[b])
        )
    return [cells[r + 3] - (flux[r + 1] - flux[r]) for r in range(n)]


def coefficients(c):
    size = jnp.abs(c)
    rest = 1.0 - size
    side = size * rest
    return c, side * rest, side * size


def chosen(flag, shape, ghost, edge):
    return jnp.where(jnp.full(shape, flag, jnp.int32) != 0, ghost, edge)


def tree(op, x):
    parts = [x[8 * i : 8 * i + 8] for i in range(16)]
    while len(parts) > 1:
        parts = [op(p, q) for p, q in zip(parts[::2], parts[1::2])]
    value = parts[0]
    for shift in (4, 2, 1):
        value = op(value, pltpu.roll(value, shift, 0))
    return value


FILL_AT = (2, 7, 12)
PHASE_AT = ((8, 15), (8, 15))
TILES_A_STEP = 3
ORDER = [(s, f) for s in range(3) for f in range(NF)]


def advance_kernel(devices, row, sel, fields, speeds, tiles, dest, fill, *refs):
    out, tiles_out, fill_out = refs[:3]
    (F, S, T, ST, O, SP0, SP1, SP2, C0, C1, C2), rest = refs[3:14], refs[14:]
    pools = [rest[6 * s : 6 * s + 6] for s in range(3)]
    R, rest = rest[18:24], rest[24:]
    (TL, G, INV, INVS), B0, B1, B2, rest = rest[:4], rest[4:6], rest[6:8], rest[8:10], rest[10:]
    (in_sem, face_send, face_recv, sp_send, sp_recv, mv_send, mv_recv, out_sem) = rest[:8]
    (inv_sem, tile_send, tile_recv, own_sem, all_send, all_recv) = rest[8:]

    gx, gy = lax.axis_index("gx"), lax.axis_index("gy")
    me = gx * row + gy
    core = lax.rem(gy, 2)
    gz, yc, y = gy // 8, lax.rem(gy, 8), lax.rem(gy // 2, 4)

    def along_x(k):
        x = lax.rem(gx + k, 4)
        return x, (x, gy)

    def along_z(k):
        z = lax.rem(gz + k, 4)
        return z, (gx, z * 8 + yc)

    def along_yc(k):
        n = lax.rem(yc + k, 8)
        return n, (gx, gz * 8 + n)

    def along_y(k):
        n = lax.rem(y + k, 4)
        return n, (gx, gz * 8 + n * 2 + core)

    def device(d):
        d = lax.rem(d + devices, devices)
        return (d // row, lax.rem(d, row))

    peer = device(me + 1 - 2 * core)

    loads = [
        pltpu.make_async_copy(
            fields.at[:, :, :, pl.ds(q * 128, 128)], F.at[:, :, pl.ds(q * 32, 32), :], in_sem.at[q]
        )
        for q in range(8)
    ] + [
        pltpu.make_async_copy(
            speeds.at[:, :, :, pl.ds(q * 128, 128)],
            S.at[:, :, pl.ds(q * 32, 32), :],
            in_sem.at[8 + q],
        )
        for q in range(8)
    ]
    tile_load = pltpu.make_async_copy(tiles, TL, in_sem.at[16])
    for load in loads + [tile_load]:
        load.start()

    barrier = pltpu.get_barrier_semaphore()
    greeted = [device(me + offset) for offset in (-2, -1, 1, 2)]
    greeted += [along_x(k)[1] for k in (1, 2, 3)] + [along_z(k)[1] for k in (1, 2, 3)]
    greeted += [along_yc(k)[1] for k in range(1, 8)]
    for other in greeted:
        pl.semaphore_signal(barrier, inc=1, device_id=other, device_id_type=MESH)
    pl.semaphore_wait(barrier, len(greeted))

    def remote(src, dst, send, recv, target):
        return pltpu.make_async_remote_copy(
            src_ref=src, dst_ref=dst, send_sem=send, recv_sem=recv,
            device_id=target, device_id_type=MESH,
        )

    class Exchange:
        def __init__(self, slot_at, send, recv):
            self.at, self.send, self.recv = slot_at, send, recv

        def start(self):
            own = self.at(2)
            self.far_up = remote(own, self.at(0), self.send.at[0], self.recv.at[0], device(me + 2))
            self.far_down = remote(
                own, self.at(4), self.send.at[1], self.recv.at[4], device(me - 2)
            )
            near = 1 + 2 * core
            self.near = remote(own, self.at(near), self.send.at[2], self.recv.at[near], peer)
            self.far_up.start()
            self.far_down.start()
            self.near.start()

        def forward(self):
            self.got(0)
            self.got(4)
            source, target = 4 - 4 * core, 3 - 2 * core
            self.passed = remote(
                self.at(source), self.at(target), self.send.at[3], self.recv.at[target], peer
            )
            self.passed.start()

        def got(self, slot):
            remote(
                self.at(slot), self.at(slot), self.send.at[0], self.recv.at[slot], peer
            ).wait_recv()

        def finish(self):
            self.got(1)
            self.got(3)

        def sent(self):
            for copy in (self.far_up, self.far_down, self.near, self.passed):
                copy.wait_send()

    def pairs(pool):
        return lambda slot: pool.at[pl.ds(2 * slot, 2)]

    def single(pool):
        return lambda slot: pool.at[slot]

    faces = [
        [
            Exchange(
                single(pools[s][f]) if s == 1 else pairs(pools[s][f]),
                face_send.at[s, f],
                face_recv.at[s, f],
            )
            for f in range(NF)
        ]
        for s in range(3)
    ]
    winds = [
        Exchange(at, sp_send.at[s], sp_recv.at[s])
        for s, at in enumerate((pairs(SP0), single(SP1), pairs(SP2)))
    ]

    sub = lax.broadcasted_iota(jnp.int32, (8, 128), 0)
    lane = lax.broadcasted_iota(jnp.int32, (8, 128), 1)

    def spot(b, d, h):
        return sel[b * 6 + 2 * d + h]

    def linked(b, d, h):
        return sel[12 + b * 6 + 2 * d + h]

    def pack_rows(s, f, A):
        pool = pools[s][f]
        for b in range(NB):
            for m in range(3):
                pool[4 + b, m] = A[b, f, pl.ds(m, 8, stride=32), :]
                pool[4 + b, 3 + m] = A[b, f, pl.ds(29 + m, 8, stride=32), :]

    def shift_up(x, ghost):
        return jnp.where(sub == 7, ghost, pltpu.roll(x, 7, 0))

    def shift_down(x, ghost):
        return jnp.where(sub == 0, ghost, pltpu.roll(x, 1, 0))

    def coef_rows(A, index, SP, d, C):
        def step(it, carry):
            b, c = it // 8, lax.rem(it, 8)
            base = c * 32
            own = [A[b, index, pl.ds(base + r, 8, stride=4), :] for r in range(4)]
            edge = A[b, index, pl.ds(base + 31, 1), :]
            ghost = SP[spot(b, d, 1), pl.ds(c, 1), :]
            ghost = chosen(linked(b, d, 1), (1, 128), ghost, edge)
            for r, value in enumerate(own + [shift_up(own[0], ghost)]):
                for n, part in enumerate(coefficients(value)):
                    C[it, 3 * r + n] = part
            return carry

        lax.fori_loop(0, 16, step, 0, unroll=2)

    def sweep_rows(s, f, A, C, strided):
        pool = pools[s][f]

        def step(it, carry):
            b, c = it // 8, lax.rem(it, 8)
            base = pl.multiple_of(c * 32, 32)
            own = [A[b, f, pl.ds(base + r, 8, stride=4), :] for r in range(4)]
            low_edge = A[b, f, pl.ds(base, 1), :]
            high_edge = A[b, f, pl.ds(base + 31, 1), :]
            low, high = spot(b, s, 0), spot(b, s, 1)
            low_on, high_on = linked(b, s, 0), linked(b, s, 1)
            before, after = [], []
            for m in range(3):
                ghost = chosen(low_on, (1, 128), pool[low, 3 + m, pl.ds(c, 1), :], low_edge)
                before.append(shift_down(own[m + 1], ghost))
                ghost = chosen(high_on, (1, 128), pool[high, m, pl.ds(c, 1), :], high_edge)
                after.append(shift_up(own[m], ghost))
            courant = [[C[it, 3 * r + n] for n in range(3)] for r in range(5)]
            result = ppm(before + own + after, courant)
            for r in range(4):
                if strided:
                    A[b, f, pl.ds(base + r, 8, stride=4), :] = result[r]
                else:
                    A[b, f, pl.ds(base + 8 * r, 8), :] = result[r]
            return carry

        lax.fori_loop(0, 16, step, 0, unroll=4)

    def pack_side(f):
        pool = pools[1][f]
        for o in range(4):
            at = o * 8
            for m in range(3):
                low = [T[b, f, pl.ds(m * 32 + at, 8), :] for b in range(NB)]
                high = [T[b, f, pl.ds(128 + (m + 1) * 32 + at, 8), :] for b in range(NB)]
                pool[2, m, pl.ds(at, 8), :] = jnp.where(
                    lane < 64,
                    jnp.where(lane < 32, low[0], pltpu.roll(low[1], 32, 1)),
                    jnp.where(lane >= 96, high[0], pltpu.roll(high[1], 96, 1)),
                )

    def side_rows(A, b, n, at):
        return [A[b, n, pl.ds(r * 32 + at, 8), :] for r in range(8)]

    def before_first(ghost, second):
        return chosen(second, (8, 128), pltpu.roll(ghost, 64, 1), pltpu.roll(ghost, 32, 1))

    def after_last(ghost, second):
        return chosen(second, (8, 128), pltpu.roll(ghost, 64, 1), pltpu.roll(ghost, 96, 1))

    def coef_side():
        def step(it, carry):
            b, o = it // 4, lax.rem(it, 4)
            at = pl.multiple_of(o * 8, 8)
            own = side_rows(ST, b, 0, at)
            where = spot(b, 1, 1)
            ghost = after_last(SP1[where // 2, pl.ds(at, 8), :], lax.rem(where, 2))
            ghost = chosen(linked(b, 1, 1), (8, 128), ghost, own[7])
            own.append(jnp.where(lane >= 96, ghost, pltpu.roll(own[0], 96, 1)))
            for r, value in enumerate(own):
                for n, part in enumerate(coefficients(value)):
                    C1[it, 3 * r + n] = part
            return carry

        lax.fori_loop(0, 8, step, 0, unroll=2)

    def sweep_side(f):
        pool = pools[1][f]

        def step(it, carry):
            b, o = it // 4, lax.rem(it, 4)
            at = pl.multiple_of(o * 8, 8)
            own = side_rows(T, b, f, at)
            low, high = spot(b, 1, 0), spot(b, 1, 1)
            low_on, high_on = linked(b, 1, 0), linked(b, 1, 1)
            before, after = [], []
            for m in range(3):
                ghost = before_first(pool[low // 2, m, pl.ds(at, 8), :], lax.rem(low, 2))
                ghost = chosen(low_on, (8, 128), ghost, own[0])
                before.append(jnp.where(lane < 32, ghost, pltpu.roll(own[5 + m], 32, 1)))
                ghost = after_last(pool[high // 2, m, pl.ds(at, 8), :], lax.rem(high, 2))
                ghost = chosen(high_on, (8, 128), ghost, own[7])
                after.append(jnp.where(lane >= 96, ghost, pltpu.roll(own[m], 96, 1)))
            courant = [[C1[it, 3 * r + n] for n in range(3)] for r in range(9)]
            result = ppm(before + own + after, courant)
            for r in range(8):
                T[b, f, pl.ds(r * 32 + at, 8), :] = result[r]
            return carry

        lax.fori_loop(0, 8, step, 0, unroll=2)

    def turn(f):
        def step(it, carry):
            b, e = it // 2, lax.rem(it, 2)
            rows = [F[b, f, pl.ds((2 * q + e) * 32, 32), :] for q in range(4)]
            T[b, f, pl.ds(e * 128, 128), :] = jnp.concatenate(rows, axis=0).T
            return carry

        lax.fori_loop(0, 4, step, 0, unroll=4)

    def turn_speeds():
        for n in range(2):
            def step(it, carry):
                b, e = it // 2, lax.rem(it, 2)
                rows = [
                    S[b, n + 1, pl.ds((2 * q + e) * 32 + r, 8, stride=4), :]
                    for q in range(4)
                    for r in range(4)
                ]
                ST[b, n, pl.ds(e * 128, 128), :] = jnp.concatenate(rows, axis=0).T
                return carry

            lax.fori_loop(0, 4, step, 0, unroll=4)

    def turn_back(f):
        def step(it, carry):
            b, e = it // 2, lax.rem(it, 2)
            back = T[b, f, pl.ds(pl.multiple_of(e * 128, 128), 128), :].T
            for q in range(4):
                for r in range(4):
                    R[f][2 + b, pl.ds((2 * q + e) * 32 + r, 8, stride=4), :] = back[
                        q * 32 + r * 8 : q * 32 + r * 8 + 8
                    ]
            return carry

        lax.fori_loop(0, 4, step, 0, unroll=4)

    def find_tiles():
        t = lax.broadcasted_iota(jnp.int32, (128, 128), 0)
        p = lax.broadcasted_iota(jnp.int32, (128, 128), 1)
        dests = jnp.broadcast_to(dest[...], (128, 128)).T
        fills = jnp.broadcast_to(fill[...], (128, 128)).T
        match = dests == p

        def rows(x):
            return jnp.concatenate([x] * 16, axis=0)

        first = tree(jnp.minimum, jnp.where(match, t, 128))
        last = tree(jnp.maximum, jnp.where(match, t, -1))
        second = jnp.where(last > first, last, 128)
        first_fill = tree(jnp.add, jnp.where(t == rows(first), fills, 0))
        second_fill = tree(jnp.add, jnp.where(t == rows(second), fills, 0))
        where = jnp.where(sub == 0, jnp.minimum(first, 127), jnp.minimum(second, 127))
        INV[...] = jnp.where(sub < 2, where, jnp.where(sub == 2, first_fill, second_fill))
        G[me, 0:1] = first_fill[0:1]
        G[me, 1:2] = second_fill[0:1]
        copy = pltpu.make_async_copy(INV, INVS, inv_sem)
        copy.start()
        return copy

    def pack_tiles():
        def step(i, carry):
            for n in range(8):
                for h in range(CAPT):
                    x = TL[INVS[h, i * 8 + n]]
                    moved = jnp.where(sub < 3, x + DRIFT * pltpu.roll(x, 5, 0), x)
                    live = lane < jnp.full((8, 128), INVS[2 + h, i * 8 + n], jnp.int32)
                    B0[h][i // 4, lax.rem(i, 4), n] = jnp.where(live, moved, 0.0)
            return carry

        lax.fori_loop(0, 16, step, 0)

    class Part:
        def __init__(self, size, along, source, target, send, recv, own):
            here = along(0)[0]
            self.own = pltpu.make_async_copy(source(here), target(here), own)
            self.copies, self.arrivals = [], []
            for k in range(1, size):
                n, other = along(k)
                self.copies.append(remote(source(n), target(here), send.at[k], recv.at[k], other))
                n, other = along(size - k)
                self.arrivals.append(remote(source(n), target(n), send.at[k], recv.at[k], other))

        def start(self):
            for copy in self.copies:
                copy.start()
            self.own.start()

        def finish(self):
            self.own.wait()
            for copy in self.arrivals:
                copy.wait_recv()

        def sent(self):
            for copy in self.copies:
                copy.wait_send()

    def seen(ref, axis, n, *half):
        after = (slice(None),) * (2 - axis) if half else ()
        return ref.at[(slice(None),) * axis + (n,) + after + half]

    def part(h, phase):
        axis = ((2, 0, 1), (1, 0, 2))[h][phase]
        size, along = (4, 4, 8)[axis], (along_x, along_z, along_yc)[axis]
        source = (B0, B1, B2)[phase][h]
        target, half = (tiles_out, (h,)) if phase == 2 else ((B1, B2)[phase][h], ())
        return Part(
            size, along,
            lambda n: seen(source, axis, n), lambda n: seen(target, axis, n, *half),
            tile_send.at[h, phase], tile_recv.at[h, phase], own_sem.at[h, phase],
        )

    class Fills:
        def __init__(self, n):
            size = (1, 2, 8, 32)[n]
            base = me // size * size
            mine = G.at[pl.ds(base, size)]
            self.copies, self.arrivals = [], []
            for k in (1,) if n == 0 else (1, 2, 3):
                send, recv = all_send.at[n, k], all_recv.at[n, k]
                for list_, j in ((self.copies, k), (self.arrivals, (2 if n == 0 else 4) - k)):
                    if n == 0:
                        other, start = peer, me + 1 - 2 * core
                    else:
                        at, other = (along_y, along_z, along_x)[n - 1](j)
                        start = base + (at - (y, gz, gx)[n - 1]) * size
                    where = mine if list_ is self.copies else G.at[pl.ds(start, size)]
                    list_.append(remote(mine, where, send, recv, other))

        def start(self):
            for copy in self.copies:
                copy.start()

        def finish(self):
            for copy in self.arrivals:
                copy.wait_recv()

        sent = Part.sent

    parts = [[part(h, phase) for phase in range(3)] for h in range(CAPT)]
    fill_steps = [Fills(n) for n in range(4)]

    def own_fills():
        flat = lax.broadcasted_iota(jnp.int32, (2, 128), 0) * 128
        flat = flat + lax.broadcasted_iota(jnp.int32, (2, 128), 1)
        mine = lax.broadcasted_iota(jnp.int32, (2, 128), 1) == me

        def step(i, total):
            for n in range(8):
                source = i * 8 + n
                value = jnp.sum(jnp.where(mine, G[source], 0), axis=1, keepdims=True)
                for h in range(CAPT):
                    total = jnp.where(
                        flat == source * CAPT + h,
                        jnp.broadcast_to(value[h : h + 1], (2, 128)),
                        total,
                    )
            return total

        fill_out[...] = lax.fori_loop(0, 16, step, jnp.zeros((2, 128), jnp.int32))

    for load in loads:
        load.wait()
    for b in range(NB):
        SP0[4 + b] = S[b, 0, pl.ds(0, 8, stride=32), :]
    winds[0].start()
    for f in range(NF):
        pack_rows(0, f, F)
        faces[0][f].start()
    found = find_tiles()
    fill_steps[0].start()
    turn_speeds()
    found.wait()
    tile_load.wait()
    pack_tiles()
    queue = list(parts[0][0].copies)
    for n, copy in enumerate(parts[1][0].copies):
        queue.insert(3 * n, copy)
    for h in range(CAPT):
        parts[h][0].own.start()

    def tiles_at(t):
        for h in range(CAPT):
            for phase in range(2):
                if t == PHASE_AT[h][phase]:
                    parts[h][phase].finish()
                    parts[h][phase + 1].start()

    for b in range(NB):
        SP2[4 + b] = ST[b, 1, pl.ds(0, 8, stride=32), :]
    for o in range(4):
        at = o * 8
        SP1[2, pl.ds(at, 8), :] = jnp.where(
            lane < 32,
            ST[0, 0, pl.ds(at, 8), :],
            pltpu.roll(ST[1, 0, pl.ds(at, 8), :], 32, 1),
        )
    winds[1].start()
    winds[2].start()
    winds[0].forward()
    faces[0][0].forward()
    winds[0].finish()
    coef_rows(S, 0, SP0, 0, C0)

    moves = {}
    first_of = {s: min(t for t in range(3 * NF) if ORDER[t][0] == s) for s in range(3)}
    for t in range(3 * NF):
        s, f = ORDER[t]
        if t + 1 < 3 * NF:
            after_s, after_f = ORDER[t + 1]
            faces[after_s][after_f].forward()
        if t == 1:
            winds[1].forward()
            winds[2].forward()
        if t == first_of[1]:
            winds[1].finish()
            coef_side()
        if t == first_of[2]:
            winds[2].finish()
            coef_rows(ST, 1, SP2, 2, C2)
        if t in FILL_AT:
            n = FILL_AT.index(t)
            fill_steps[n].finish()
            fill_steps[n + 1].start()
        tiles_at(t)
        faces[s][f].finish()
        if s == 0:
            sweep_rows(0, f, F, C0, False)
            turn(f)
            pack_side(f)
            faces[1][f].start()
        elif s == 1:
            sweep_side(f)
            pack_rows(2, f, T)
            faces[2][f].start()
        else:
            sweep_rows(2, f, T, C2, True)
            turn_back(f)
            own = R[f].at[pl.ds(2, 2)]
            pair = [
                remote(own, R[f].at[pl.ds(0, 2)], mv_send.at[f, 0], mv_recv.at[f, 0], device(me + 1)),
                remote(own, R[f].at[pl.ds(4, 2)], mv_send.at[f, 1], mv_recv.at[f, 1], device(me - 1)),
            ]
            for copy in pair:
                copy.start()
            moves[f] = pair
        for _ in range(TILES_A_STEP):
            if queue:
                queue.pop(0).start()

    fill_steps[3].finish()
    own_fills()
    stores = []
    for f in range(NF):
        tiles_at(3 * NF + f)
        for copy in moves[f]:
            copy.wait_recv()
        for j in range(NB):
            def step(i, carry):
                at = pl.multiple_of(i * 8, 8)
                for q in range(8):
                    O[j, f, pl.ds(at, 8), pl.ds(q * 128, 128)] = R[f][
                        sel[24 + j], pl.ds(q * 32 + at, 8), :
                    ]
                return carry

            lax.fori_loop(0, 4, step, 0, unroll=2)
        stores.append(pltpu.make_async_copy(O.at[:, f], out.at[:, f], out_sem.at[f]))
        stores[-1].start()
    for h in range(CAPT):
        parts[h][2].finish()
    for group in faces + [winds, fill_steps] + parts:
        for exchange in group:
            exchange.sent()
    for pair in moves.values():
        for copy in pair:
            copy.wait_send()
    for store in stores:
        store.wait()


def advance(fields, speeds, sel, tiles, dest, fill, devices, row):
    f32, i32 = jnp.float32, jnp.int32
    dma = pltpu.SemaphoreType.DMA
    scratch = [
        pltpu.VMEM((NB, NF, 256, 128), f32),
        pltpu.VMEM((NB, 3, 256, 128), f32),
        pltpu.VMEM((NB, NF, 256, 128), f32),
        pltpu.VMEM((NB, 2, 256, 128), f32),
        pltpu.VMEM((NB, NF, 32, 1024), f32),
        pltpu.VMEM((10, 8, 128), f32),
        pltpu.VMEM((5, 32, 128), f32),
        pltpu.VMEM((10, 8, 128), f32),
    ]
    scratch += [pltpu.VMEM((8, 27, 8, 128) if s == 1 else (16, 15, 8, 128), f32) for s in range(3)]
    for s in range(3):
        shape = (5, 3, 32, 128) if s == 1 else (10, 6, 8, 128)
        scratch += [pltpu.VMEM(shape, f32) for _ in range(NF)]
    scratch += [pltpu.VMEM((6, 256, 128), f32) for _ in range(NF)]
    scratch += [
        pltpu.VMEM((128, 8, 128), f32),
        pltpu.VMEM((128, CAPT, 128), i32),
        pltpu.VMEM((8, 128), i32),
        pltpu.SMEM((8, 128), i32),
    ]
    scratch += [pltpu.VMEM((4, 4, 8, 8, 128), f32) for _ in range(3 * CAPT)]
    scratch += [
        dma((17,)), dma((3, NF, 4)), dma((3, NF, 5)), dma((3, 4)), dma((3, 5)),
        dma((NF, 2)), dma((NF, 2)), dma((NF,)),
        dma(()), dma((CAPT, 3, 8)), dma((CAPT, 3, 8)), dma((CAPT, 3)), dma((4, 4)), dma((4, 4)),
    ]
    return pl.pallas_call(
        functools.partial(advance_kernel, devices, row),
        out_shape=(
            jax.ShapeDtypeStruct(fields.shape, f32),
            jax.ShapeDtypeStruct((4, 4, 8, CAPT, 8, 128), f32),
            jax.ShapeDtypeStruct((CAPT, 128), i32),
        ),
        in_specs=[
            pl.BlockSpec(memory_space=pltpu.SMEM),
            pl.BlockSpec(memory_space=pltpu.HBM),
            pl.BlockSpec(memory_space=pltpu.HBM),
            pl.BlockSpec(memory_space=pltpu.HBM),
            pl.BlockSpec(memory_space=pltpu.VMEM),
            pl.BlockSpec(memory_space=pltpu.VMEM),
        ],
        out_specs=(
            pl.BlockSpec(memory_space=pl.ANY),
            pl.BlockSpec(memory_space=pl.ANY),
            pl.BlockSpec(memory_space=pltpu.VMEM),
        ),
        scratch_shapes=scratch,
        name="advance_blocks",
        compiler_params=pltpu.CompilerParams(
            collective_id=0, has_side_effects=True, vmem_limit_bytes=60 * 1024 * 1024
        ),
    )(sel, fields, speeds, tiles, dest, fill)


def body(fields, speeds, neighbours, block_order, tiles, tile_fill, tile_dest):
    row = lax.axis_size("gy")
    devices = lax.axis_size(AXES)
    me = lax.axis_index(AXES)
    first_block = me * NB

    links = lax.dynamic_slice_in_dim(neighbours, first_block, NB).reshape(-1)
    spots = jnp.clip((links // 2 - me + 2) * 2 + links % 2, 0, 9)
    incoming = lax.dynamic_slice_in_dim(block_order, first_block, NB)
    picks = jnp.clip((incoming // 2 - me + 1) * 2 + incoming % 2, 0, 5)
    sel = jnp.concatenate([spots, (links >= 0).astype(jnp.int32), picks])

    blocks_out, tiles_out, fill_out = advance(
        fields, speeds, sel, tiles, tile_dest.reshape(1, -1), tile_fill.reshape(1, -1), devices, row
    )
    return blocks_out, tiles_out.reshape((-1,) + tiles.shape[1:]), fill_out.reshape(-1)


def solution(mesh):
    blocks = P(AXES, None, None, None)
    return jax.shard_map(
        body,
        mesh=mesh,
        in_specs=(blocks, blocks, P(), P(), P(AXES, None, None), P(AXES), P(AXES, None)),
        out_specs=(blocks, P(AXES, None, None), P(AXES)),
        check_vma=False,
    )
```

```python
import functools

import jax
import jax.numpy as jnp
from jax import lax
from jax.experimental import pallas as pl
from jax.experimental.pallas import tpu as pltpu
from jax.sharding import PartitionSpec as P

MESH = pl.DeviceIdType.MESH
NF = 6
NB = 2
CAPT = 2
DRIFT = 0.5
AXES = ("gx", "gy")


def ppm(cells, courant):
    n = len(cells) - 6
    delta = [cells[i + 1] - cells[i] for i in range(n + 5)]
    right, left = {}, {}
    for i in range(1, n + 4):
        step = 0.5 * delta[i] + (1.0 / 12.0) * (delta[i - 1] - delta[i + 1])
        step = jnp.minimum(
            jnp.maximum(step, jnp.minimum(delta[i], 0.0)), jnp.maximum(delta[i], 0.0)
        )
        right[i], left[i + 1] = step, delta[i] - step
    up, down = {}, {}
    for i in range(2, n + 4):
        r, l = right[i], left[i]
        r2, l2 = r + r, l + l
        up[i] = jnp.maximum(jnp.minimum(r, l2), 0.0) + jnp.minimum(jnp.maximum(r, l2), 0.0)
        down[i] = jnp.maximum(jnp.minimum(l, r2), 0.0) + jnp.minimum(jnp.maximum(l, r2), 0.0)
    flux = []
    for f in range(n + 1):
        c, ca, cb = courant[f]
        a, b = f + 2, f + 3
        wind = c > 0.0
        flux.append(
            c * jnp.where(wind, cells[a], cells[b])
            + ca * jnp.where(wind, up[a], down[b])
            + cb * jnp.where(wind, down[a], up[b])
        )
    return [cells[r + 3] - (flux[r + 1] - flux[r]) for r in range(n)]


def coefficients(c):
    size = jnp.abs(c)
    rest = 1.0 - size
    side = size * rest
    return c, side * rest, side * size


def chosen(flag, shape, ghost, edge):
    return jnp.where(jnp.full(shape, flag, jnp.int32) != 0, ghost, edge)


def tree(op, x):
    parts = [x[8 * i : 8 * i + 8] for i in range(16)]
    while len(parts) > 1:
        parts = [op(p, q) for p, q in zip(parts[::2], parts[1::2])]
    value = parts[0]
    for shift in (4, 2, 1):
        value = op(value, pltpu.roll(value, shift, 0))
    return value


FILL_AT = (2, 7, 12)
PHASE_AT = ((8, 15), (8, 15))
TILES_A_STEP = 3
ORDER = [(s, f) for s in range(3) for f in range(NF)]


def advance_kernel(devices, row, neighbours, order, fields, speeds, tiles, dest, fill, *refs):
    out, tiles_out, fill_out = refs[:3]
    (F, S, T, ST, O, SP0, SP1, SP2, C0, C1, C2), rest = refs[3:14], refs[14:]
    pools = [rest[6 * s : 6 * s + 6] for s in range(3)]
    R, rest = rest[18:24], rest[24:]
    (TL, G, INV, INVS), B0, B1, B2, rest = rest[:4], rest[4:6], rest[6:8], rest[8:10], rest[10:]
    (in_sem, face_send, face_recv, sp_send, sp_recv, mv_send, mv_recv, out_sem) = rest[:8]
    (inv_sem, tile_send, tile_recv, own_sem, all_send, all_recv) = rest[8:]

    gx, gy = lax.axis_index("gx"), lax.axis_index("gy")
    me = gx * row + gy
    core = lax.rem(gy, 2)
    gz, yc, y = gy // 8, lax.rem(gy, 8), lax.rem(gy // 2, 4)

    def along_x(k):
        x = lax.rem(gx + k, 4)
        return x, (x, gy)

    def along_z(k):
        z = lax.rem(gz + k, 4)
        return z, (gx, z * 8 + yc)

    def along_yc(k):
        n = lax.rem(yc + k, 8)
        return n, (gx, gz * 8 + n)

    def along_y(k):
        n = lax.rem(y + k, 4)
        return n, (gx, gz * 8 + n * 2 + core)

    def device(d):
        d = lax.rem(d + devices, devices)
        return (d // row, lax.rem(d, row))

    peer = device(me + 1 - 2 * core)

    loads = [
        pltpu.make_async_copy(
            fields.at[:, :, :, pl.ds(q * 128, 128)], F.at[:, :, pl.ds(q * 32, 32), :], in_sem.at[q]
        )
        for q in range(8)
    ] + [
        pltpu.make_async_copy(
            speeds.at[:, :, :, pl.ds(q * 128, 128)],
            S.at[:, :, pl.ds(q * 32, 32), :],
            in_sem.at[8 + q],
        )
        for q in range(8)
    ]
    tile_load = pltpu.make_async_copy(tiles, TL, in_sem.at[16])
    for load in loads + [tile_load]:
        load.start()

    barrier = pltpu.get_barrier_semaphore()
    greeted = [device(me + offset) for offset in (-2, -1, 1, 2)]
    greeted += [along_x(k)[1] for k in (1, 2, 3)] + [along_z(k)[1] for k in (1, 2, 3)]
    greeted += [along_yc(k)[1] for k in range(1, 8)]
    for other in greeted:
        pl.semaphore_signal(barrier, inc=1, device_id=other, device_id_type=MESH)
    pl.semaphore_wait(barrier, len(greeted))

    def remote(src, dst, send, recv, target):
        return pltpu.make_async_remote_copy(
            src_ref=src, dst_ref=dst, send_sem=send, recv_sem=recv,
            device_id=target, device_id_type=MESH,
        )

    class Exchange:
        def __init__(self, slot_at, send, recv):
            self.at, self.send, self.recv = slot_at, send, recv

        def start(self):
            own = self.at(2)
            self.far_up = remote(own, self.at(0), self.send.at[0], self.recv.at[0], device(me + 2))
            self.far_down = remote(
                own, self.at(4), self.send.at[1], self.recv.at[4], device(me - 2)
            )
            near = 1 + 2 * core
            self.near = remote(own, self.at(near), self.send.at[2], self.recv.at[near], peer)
            self.far_up.start()
            self.far_down.start()
            self.near.start()

        def forward(self):
            self.got(0)
            self.got(4)
            source, target = 4 - 4 * core, 3 - 2 * core
            self.passed = remote(
                self.at(source), self.at(target), self.send.at[3], self.recv.at[target], peer
            )
            self.passed.start()

        def got(self, slot):
            remote(
                self.at(slot), self.at(slot), self.send.at[0], self.recv.at[slot], peer
            ).wait_recv()

        def finish(self):
            self.got(1)
            self.got(3)

        def sent(self):
            for copy in (self.far_up, self.far_down, self.near, self.passed):
                copy.wait_send()

    def pairs(pool):
        return lambda slot: pool.at[pl.ds(2 * slot, 2)]

    def single(pool):
        return lambda slot: pool.at[slot]

    faces = [
        [
            Exchange(
                single(pools[s][f]) if s == 1 else pairs(pools[s][f]),
                face_send.at[s, f],
                face_recv.at[s, f],
            )
            for f in range(NF)
        ]
        for s in range(3)
    ]
    winds = [
        Exchange(at, sp_send.at[s], sp_recv.at[s])
        for s, at in enumerate((pairs(SP0), single(SP1), pairs(SP2)))
    ]

    sub = lax.broadcasted_iota(jnp.int32, (8, 128), 0)
    lane = lax.broadcasted_iota(jnp.int32, (8, 128), 1)

    def place(n, reach):
        found = (jnp.right_shift(n, 1) - me + reach) * 2 + jnp.bitwise_and(n, 1)
        return jnp.minimum(jnp.maximum(found, 0), 4 * reach + 1)

    def spot(b, d, h):
        return place(neighbours[2 * d + h, me * NB + b], 2)

    def linked(b, d, h):
        return (neighbours[2 * d + h, me * NB + b] >= 0).astype(jnp.int32)

    def pack_rows(s, f, A):
        pool = pools[s][f]
        for b in range(NB):
            for m in range(3):
                pool[4 + b, m] = A[b, f, pl.ds(m, 8, stride=32), :]
                pool[4 + b, 3 + m] = A[b, f, pl.ds(29 + m, 8, stride=32), :]

    def shift_up(x, ghost):
        return jnp.where(sub == 7, ghost, pltpu.roll(x, 7, 0))

    def shift_down(x, ghost):
        return jnp.where(sub == 0, ghost, pltpu.roll(x, 1, 0))

    def coef_rows(A, index, SP, d, C):
        def step(it, carry):
            b, c = it // 8, lax.rem(it, 8)
            base = c * 32
            own = [A[b, index, pl.ds(base + r, 8, stride=4), :] for r in range(4)]
            edge = A[b, index, pl.ds(base + 31, 1), :]
            ghost = SP[spot(b, d, 1), pl.ds(c, 1), :]
            ghost = chosen(linked(b, d, 1), (1, 128), ghost, edge)
            for r, value in enumerate(own + [shift_up(own[0], ghost)]):
                for n, part in enumerate(coefficients(value)):
                    C[it, 3 * r + n] = part
            return carry

        lax.fori_loop(0, 16, step, 0, unroll=2)

    def sweep_rows(s, f, A, C, strided):
        pool = pools[s][f]

        def step(it, carry):
            b, c = it // 8, lax.rem(it, 8)
            base = pl.multiple_of(c * 32, 32)
            own = [A[b, f, pl.ds(base + r, 8, stride=4), :] for r in range(4)]
            low_edge = A[b, f, pl.ds(base, 1), :]
            high_edge = A[b, f, pl.ds(base + 31, 1), :]
            low, high = spot(b, s, 0), spot(b, s, 1)
            low_on, high_on = linked(b, s, 0), linked(b, s, 1)
            before, after = [], []
            for m in range(3):
                ghost = chosen(low_on, (1, 128), pool[low, 3 + m, pl.ds(c, 1), :], low_edge)
                before.append(shift_down(own[m + 1], ghost))
                ghost = chosen(high_on, (1, 128), pool[high, m, pl.ds(c, 1), :], high_edge)
                after.append(shift_up(own[m], ghost))
            courant = [[C[it, 3 * r + n] for n in range(3)] for r in range(5)]
            result = ppm(before + own + after, courant)
            for r in range(4):
                if strided:
                    A[b, f, pl.ds(base + r, 8, stride=4), :] = result[r]
                else:
                    A[b, f, pl.ds(base + 8 * r, 8), :] = result[r]
            return carry

        lax.fori_loop(0, 16, step, 0, unroll=4)

    def pack_side(f):
        pool = pools[1][f]
        for o in range(4):
            at = o * 8
            for m in range(3):
                low = [T[b, f, pl.ds(m * 32 + at, 8), :] for b in range(NB)]
                high = [T[b, f, pl.ds(128 + (m + 1) * 32 + at, 8), :] for b in range(NB)]
                pool[2, m, pl.ds(at, 8), :] = jnp.where(
                    lane < 64,
                    jnp.where(lane < 32, low[0], pltpu.roll(low[1], 32, 1)),
                    jnp.where(lane >= 96, high[0], pltpu.roll(high[1], 96, 1)),
                )

    def side_rows(A, b, n, at):
        return [A[b, n, pl.ds(r * 32 + at, 8), :] for r in range(8)]

    def before_first(ghost, second):
        return chosen(second, (8, 128), pltpu.roll(ghost, 64, 1), pltpu.roll(ghost, 32, 1))

    def after_last(ghost, second):
        return chosen(second, (8, 128), pltpu.roll(ghost, 64, 1), pltpu.roll(ghost, 96, 1))

    def coef_side():
        def step(it, carry):
            b, o = it // 4, lax.rem(it, 4)
            at = pl.multiple_of(o * 8, 8)
            own = side_rows(ST, b, 0, at)
            where = spot(b, 1, 1)
            ghost = after_last(SP1[where // 2, pl.ds(at, 8), :], lax.rem(where, 2))
            ghost = chosen(linked(b, 1, 1), (8, 128), ghost, own[7])
            own.append(jnp.where(lane >= 96, ghost, pltpu.roll(own[0], 96, 1)))
            for r, value in enumerate(own):
                for n, part in enumerate(coefficients(value)):
                    C1[it, 3 * r + n] = part
            return carry

        lax.fori_loop(0, 8, step, 0, unroll=2)

    def sweep_side(f):
        pool = pools[1][f]

        def step(it, carry):
            b, o = it // 4, lax.rem(it, 4)
            at = pl.multiple_of(o * 8, 8)
            own = side_rows(T, b, f, at)
            low, high = spot(b, 1, 0), spot(b, 1, 1)
            low_on, high_on = linked(b, 1, 0), linked(b, 1, 1)
            before, after = [], []
            for m in range(3):
                ghost = before_first(pool[low // 2, m, pl.ds(at, 8), :], lax.rem(low, 2))
                ghost = chosen(low_on, (8, 128), ghost, own[0])
                before.append(jnp.where(lane < 32, ghost, pltpu.roll(own[5 + m], 32, 1)))
                ghost = after_last(pool[high // 2, m, pl.ds(at, 8), :], lax.rem(high, 2))
                ghost = chosen(high_on, (8, 128), ghost, own[7])
                after.append(jnp.where(lane >= 96, ghost, pltpu.roll(own[m], 96, 1)))
            courant = [[C1[it, 3 * r + n] for n in range(3)] for r in range(9)]
            result = ppm(before + own + after, courant)
            for r in range(8):
                T[b, f, pl.ds(r * 32 + at, 8), :] = result[r]
            return carry

        lax.fori_loop(0, 8, step, 0, unroll=2)

    def turn(f):
        def step(it, carry):
            b, e = it // 2, lax.rem(it, 2)
            rows = [F[b, f, pl.ds((2 * q + e) * 32, 32), :] for q in range(4)]
            T[b, f, pl.ds(e * 128, 128), :] = jnp.concatenate(rows, axis=0).T
            return carry

        lax.fori_loop(0, 4, step, 0, unroll=4)

    def turn_speeds():
        for n in range(2):
            def step(it, carry):
                b, e = it // 2, lax.rem(it, 2)
                rows = [
                    S[b, n + 1, pl.ds((2 * q + e) * 32 + r, 8, stride=4), :]
                    for q in range(4)
                    for r in range(4)
                ]
                ST[b, n, pl.ds(e * 128, 128), :] = jnp.concatenate(rows, axis=0).T
                return carry

            lax.fori_loop(0, 4, step, 0, unroll=4)

    def turn_back(f):
        def step(it, carry):
            b, e = it // 2, lax.rem(it, 2)
            back = T[b, f, pl.ds(pl.multiple_of(e * 128, 128), 128), :].T
            for q in range(4):
                for r in range(4):
                    R[f][2 + b, pl.ds((2 * q + e) * 32 + r, 8, stride=4), :] = back[
                        q * 32 + r * 8 : q * 32 + r * 8 + 8
                    ]
            return carry

        lax.fori_loop(0, 4, step, 0, unroll=4)

    def find_tiles():
        t = lax.broadcasted_iota(jnp.int32, (128, 128), 0)
        p = lax.broadcasted_iota(jnp.int32, (128, 128), 1)
        dests = jnp.broadcast_to(dest[...], (128, 128)).T
        fills = jnp.broadcast_to(fill[...], (128, 128)).T
        match = dests == p

        def rows(x):
            return jnp.concatenate([x] * 16, axis=0)

        first = tree(jnp.minimum, jnp.where(match, t, 128))
        last = tree(jnp.maximum, jnp.where(match, t, -1))
        second = jnp.where(last > first, last, 128)
        first_fill = tree(jnp.add, jnp.where(t == rows(first), fills, 0))
        second_fill = tree(jnp.add, jnp.where(t == rows(second), fills, 0))
        where = jnp.where(sub == 0, jnp.minimum(first, 127), jnp.minimum(second, 127))
        INV[...] = jnp.where(sub < 2, where, jnp.where(sub == 2, first_fill, second_fill))
        G[me, 0:1] = first_fill[0:1]
        G[me, 1:2] = second_fill[0:1]
        copy = pltpu.make_async_copy(INV, INVS, inv_sem)
        copy.start()
        return copy

    def pack_tiles():
        def step(i, carry):
            for n in range(8):
                for h in range(CAPT):
                    x = TL[INVS[h, i * 8 + n]]
                    moved = jnp.where(sub < 3, x + DRIFT * pltpu.roll(x, 5, 0), x)
                    live = lane < jnp.full((8, 128), INVS[2 + h, i * 8 + n], jnp.int32)
                    B0[h][i // 4, lax.rem(i, 4), n] = jnp.where(live, moved, 0.0)
            return carry

        lax.fori_loop(0, 16, step, 0)

    class Part:
        def __init__(self, size, along, source, target, send, recv, own):
            here = along(0)[0]
            self.own = pltpu.make_async_copy(source(here), target(here), own)
            self.copies, self.arrivals = [], []
            for k in range(1, size):
                n, other = along(k)
                self.copies.append(remote(source(n), target(here), send.at[k], recv.at[k], other))
                n, other = along(size - k)
                self.arrivals.append(remote(source(n), target(n), send.at[k], recv.at[k], other))

        def start(self):
            for copy in self.copies:
                copy.start()
            self.own.start()

        def finish(self):
            self.own.wait()
            for copy in self.arrivals:
                copy.wait_recv()

        def sent(self):
            for copy in self.copies:
                copy.wait_send()

    def seen(ref, axis, n, *half):
        after = (slice(None),) * (2 - axis) if half else ()
        return ref.at[(slice(None),) * axis + (n,) + after + half]

    def part(h, phase):
        axis = ((2, 0, 1), (1, 0, 2))[h][phase]
        size, along = (4, 4, 8)[axis], (along_x, along_z, along_yc)[axis]
        source = (B0, B1, B2)[phase][h]
        target, half = (tiles_out, (h,)) if phase == 2 else ((B1, B2)[phase][h], ())
        return Part(
            size, along,
            lambda n: seen(source, axis, n), lambda n: seen(target, axis, n, *half),
            tile_send.at[h, phase], tile_recv.at[h, phase], own_sem.at[h, phase],
        )

    class Fills:
        def __init__(self, n):
            size = (1, 2, 8, 32)[n]
            base = me // size * size
            mine = G.at[pl.ds(base, size)]
            self.copies, self.arrivals = [], []
            for k in (1,) if n == 0 else (1, 2, 3):
                send, recv = all_send.at[n, k], all_recv.at[n, k]
                for list_, j in ((self.copies, k), (self.arrivals, (2 if n == 0 else 4) - k)):
                    if n == 0:
                        other, start = peer, me + 1 - 2 * core
                    else:
                        at, other = (along_y, along_z, along_x)[n - 1](j)
                        start = base + (at - (y, gz, gx)[n - 1]) * size
                    where = mine if list_ is self.copies else G.at[pl.ds(start, size)]
                    list_.append(remote(mine, where, send, recv, other))

        def start(self):
            for copy in self.copies:
                copy.start()

        def finish(self):
            for copy in self.arrivals:
                copy.wait_recv()

        sent = Part.sent

    parts = [[part(h, phase) for phase in range(3)] for h in range(CAPT)]
    fill_steps = [Fills(n) for n in range(4)]

    def own_fills():
        flat = lax.broadcasted_iota(jnp.int32, (2, 128), 0) * 128
        flat = flat + lax.broadcasted_iota(jnp.int32, (2, 128), 1)
        mine = lax.broadcasted_iota(jnp.int32, (2, 128), 1) == me

        def step(i, total):
            for n in range(8):
                source = i * 8 + n
                value = jnp.sum(jnp.where(mine, G[source], 0), axis=1, keepdims=True)
                for h in range(CAPT):
                    total = jnp.where(
                        flat == source * CAPT + h,
                        jnp.broadcast_to(value[h : h + 1], (2, 128)),
                        total,
                    )
            return total

        fill_out[...] = lax.fori_loop(0, 16, step, jnp.zeros((2, 128), jnp.int32))

    for load in loads:
        load.wait()
    for b in range(NB):
        SP0[4 + b] = S[b, 0, pl.ds(0, 8, stride=32), :]
    winds[0].start()
    for f in range(NF):
        pack_rows(0, f, F)
        faces[0][f].start()
    found = find_tiles()
    fill_steps[0].start()
    turn_speeds()
    found.wait()
    tile_load.wait()
    pack_tiles()
    queue = list(parts[0][0].copies)
    for n, copy in enumerate(parts[1][0].copies):
        queue.insert(3 * n, copy)
    for h in range(CAPT):
        parts[h][0].own.start()

    def tiles_at(t):
        for h in range(CAPT):
            for phase in range(2):
                if t == PHASE_AT[h][phase]:
                    parts[h][phase].finish()
                    parts[h][phase + 1].start()

    for b in range(NB):
        SP2[4 + b] = ST[b, 1, pl.ds(0, 8, stride=32), :]
    for o in range(4):
        at = o * 8
        SP1[2, pl.ds(at, 8), :] = jnp.where(
            lane < 32,
            ST[0, 0, pl.ds(at, 8), :],
            pltpu.roll(ST[1, 0, pl.ds(at, 8), :], 32, 1),
        )
    winds[1].start()
    winds[2].start()
    winds[0].forward()
    faces[0][0].forward()
    winds[0].finish()
    coef_rows(S, 0, SP0, 0, C0)

    moves = {}
    first_of = {s: min(t for t in range(3 * NF) if ORDER[t][0] == s) for s in range(3)}
    for t in range(3 * NF):
        s, f = ORDER[t]
        if t + 1 < 3 * NF:
            after_s, after_f = ORDER[t + 1]
            faces[after_s][after_f].forward()
        if t == 1:
            winds[1].forward()
            winds[2].forward()
        if t == first_of[1]:
            winds[1].finish()
            coef_side()
        if t == first_of[2]:
            winds[2].finish()
            coef_rows(ST, 1, SP2, 2, C2)
        if t in FILL_AT:
            n = FILL_AT.index(t)
            fill_steps[n].finish()
            fill_steps[n + 1].start()
        tiles_at(t)
        faces[s][f].finish()
        if s == 0:
            sweep_rows(0, f, F, C0, False)
            turn(f)
            pack_side(f)
            faces[1][f].start()
        elif s == 1:
            sweep_side(f)
            pack_rows(2, f, T)
            faces[2][f].start()
        else:
            sweep_rows(2, f, T, C2, True)
            turn_back(f)
            own = R[f].at[pl.ds(2, 2)]
            pair = [
                remote(own, R[f].at[pl.ds(0, 2)], mv_send.at[f, 0], mv_recv.at[f, 0], device(me + 1)),
                remote(own, R[f].at[pl.ds(4, 2)], mv_send.at[f, 1], mv_recv.at[f, 1], device(me - 1)),
            ]
            for copy in pair:
                copy.start()
            moves[f] = pair
        for _ in range(TILES_A_STEP):
            if queue:
                queue.pop(0).start()

    fill_steps[3].finish()
    own_fills()
    stores = []
    for f in range(NF):
        tiles_at(3 * NF + f)
        for copy in moves[f]:
            copy.wait_recv()
        for j in range(NB):
            def step(i, carry):
                at = pl.multiple_of(i * 8, 8)
                for q in range(8):
                    O[j, f, pl.ds(at, 8), pl.ds(q * 128, 128)] = R[f][
                        place(order[me * NB + j], 1), pl.ds(q * 32 + at, 8), :
                    ]
                return carry

            lax.fori_loop(0, 4, step, 0, unroll=2)
        stores.append(pltpu.make_async_copy(O.at[:, f], out.at[:, f], out_sem.at[f]))
        stores[-1].start()
    for h in range(CAPT):
        parts[h][2].finish()
    for group in faces + [winds, fill_steps] + parts:
        for exchange in group:
            exchange.sent()
    for pair in moves.values():
        for copy in pair:
            copy.wait_send()
    for store in stores:
        store.wait()


def advance(fields, speeds, neighbours, order, tiles, dest, fill, devices, row):
    f32, i32 = jnp.float32, jnp.int32
    dma = pltpu.SemaphoreType.DMA
    scratch = [
        pltpu.VMEM((NB, NF, 256, 128), f32),
        pltpu.VMEM((NB, 3, 256, 128), f32),
        pltpu.VMEM((NB, NF, 256, 128), f32),
        pltpu.VMEM((NB, 2, 256, 128), f32),
        pltpu.VMEM((NB, NF, 32, 1024), f32),
        pltpu.VMEM((10, 8, 128), f32),
        pltpu.VMEM((5, 32, 128), f32),
        pltpu.VMEM((10, 8, 128), f32),
    ]
    scratch += [pltpu.VMEM((8, 27, 8, 128) if s == 1 else (16, 15, 8, 128), f32) for s in range(3)]
    for s in range(3):
        shape = (5, 3, 32, 128) if s == 1 else (10, 6, 8, 128)
        scratch += [pltpu.VMEM(shape, f32) for _ in range(NF)]
    scratch += [pltpu.VMEM((6, 256, 128), f32) for _ in range(NF)]
    scratch += [
        pltpu.VMEM((128, 8, 128), f32),
        pltpu.VMEM((128, CAPT, 128), i32),
        pltpu.VMEM((8, 128), i32),
        pltpu.SMEM((8, 128), i32),
    ]
    scratch += [pltpu.VMEM((4, 4, 8, 8, 128), f32) for _ in range(3 * CAPT)]
    scratch += [
        dma((17,)), dma((3, NF, 4)), dma((3, NF, 5)), dma((3, 4)), dma((3, 5)),
        dma((NF, 2)), dma((NF, 2)), dma((NF,)),
        dma(()), dma((CAPT, 3, 8)), dma((CAPT, 3, 8)), dma((CAPT, 3)), dma((4, 4)), dma((4, 4)),
    ]
    return pl.pallas_call(
        functools.partial(advance_kernel, devices, row),
        out_shape=(
            jax.ShapeDtypeStruct(fields.shape, f32),
            jax.ShapeDtypeStruct((4, 4, 8, CAPT, 8, 128), f32),
            jax.ShapeDtypeStruct((CAPT, 128), i32),
        ),
        in_specs=[
            pl.BlockSpec(memory_space=pltpu.SMEM),
            pl.BlockSpec(memory_space=pltpu.SMEM),
            pl.BlockSpec(memory_space=pltpu.HBM),
            pl.BlockSpec(memory_space=pltpu.HBM),
            pl.BlockSpec(memory_space=pltpu.HBM),
            pl.BlockSpec(memory_space=pltpu.VMEM),
            pl.BlockSpec(memory_space=pltpu.VMEM),
        ],
        out_specs=(
            pl.BlockSpec(memory_space=pl.ANY),
            pl.BlockSpec(memory_space=pl.ANY),
            pl.BlockSpec(memory_space=pltpu.VMEM),
        ),
        scratch_shapes=scratch,
        name="advance_blocks",
        compiler_params=pltpu.CompilerParams(
            collective_id=0, has_side_effects=True, vmem_limit_bytes=60 * 1024 * 1024
        ),
    )(neighbours, order, fields, speeds, tiles, dest, fill)


def body(fields, speeds, neighbours, block_order, tiles, tile_fill, tile_dest):
    row = lax.axis_size("gy")
    devices = lax.axis_size(AXES)
    blocks_out, tiles_out, fill_out = advance(
        fields, speeds, neighbours.T, block_order, tiles,
        tile_dest.reshape(1, -1), tile_fill.reshape(1, -1), devices, row,
    )
    return blocks_out, tiles_out.reshape((-1,) + tiles.shape[1:]), fill_out.reshape(-1)


def solution(mesh):
    blocks = P(AXES, None, None, None)
    return jax.shard_map(
        body,
        mesh=mesh,
        in_specs=(blocks, blocks, P(), P(), P(AXES, None, None), P(AXES), P(AXES, None)),
        out_specs=(blocks, P(AXES, None, None), P(AXES)),
        check_vma=False,
    )
```

```python
import functools

import jax
import jax.numpy as jnp
from jax import lax
from jax.experimental import pallas as pl
from jax.experimental.pallas import tpu as pltpu
from jax.sharding import PartitionSpec as P

MESH = pl.DeviceIdType.MESH
NF = 6
NB = 2
CAPT = 2
DRIFT = 0.5
AXES = ("gx", "gy")


def ppm(cells, courant):
    n = len(cells) - 6
    delta = [cells[i + 1] - cells[i] for i in range(n + 5)]
    right, left = {}, {}
    for i in range(1, n + 4):
        step = 0.5 * delta[i] + (1.0 / 12.0) * (delta[i - 1] - delta[i + 1])
        step = jnp.minimum(
            jnp.maximum(step, jnp.minimum(delta[i], 0.0)), jnp.maximum(delta[i], 0.0)
        )
        right[i], left[i + 1] = step, delta[i] - step
    up, down = {}, {}
    for i in range(2, n + 4):
        r, l = right[i], left[i]
        r2, l2 = r + r, l + l
        up[i] = jnp.maximum(jnp.minimum(r, l2), 0.0) + jnp.minimum(jnp.maximum(r, l2), 0.0)
        down[i] = jnp.maximum(jnp.minimum(l, r2), 0.0) + jnp.minimum(jnp.maximum(l, r2), 0.0)
    flux = []
    for f in range(n + 1):
        c, ca, cb = courant[f]
        a, b = f + 2, f + 3
        wind = c > 0.0
        flux.append(
            c * jnp.where(wind, cells[a], cells[b])
            + ca * jnp.where(wind, up[a], down[b])
            + cb * jnp.where(wind, down[a], up[b])
        )
    return [cells[r + 3] - (flux[r + 1] - flux[r]) for r in range(n)]


def coefficients(c):
    size = jnp.abs(c)
    rest = 1.0 - size
    side = size * rest
    return c, side * rest, side * size


def chosen(flag, shape, ghost, edge):
    return jnp.where(jnp.full(shape, flag, jnp.int32) != 0, ghost, edge)


def tree(op, x):
    parts = [x[8 * i : 8 * i + 8] for i in range(16)]
    while len(parts) > 1:
        parts = [op(p, q) for p, q in zip(parts[::2], parts[1::2])]
    value = parts[0]
    for shift in (4, 2, 1):
        value = op(value, pltpu.roll(value, shift, 0))
    return value


FILL_AT = (2, 7, 12)
PHASE_AT = ((8, 15), (8, 15))
TILES_A_STEP = 3
ORDER = [(s, f) for s in range(3) for f in range(NF)]


def advance_kernel(devices, row, neighbours, order, fields, speeds, tiles, dest, fill, *refs):
    out, tiles_out, fill_out = refs[:3]
    (F, S, T, ST, O, SP0, SP1, SP2, C0, C1, C2), rest = refs[3:14], refs[14:]
    pools = [rest[6 * s : 6 * s + 6] for s in range(3)]
    R, rest = rest[18:24], rest[24:]
    (TL, G, INV, INVS), B0, B1, B2, rest = rest[:4], rest[4:6], rest[6:8], rest[8:10], rest[10:]
    (in_sem, face_send, face_recv, sp_send, sp_recv, mv_send, mv_recv, out_sem) = rest[:8]
    (inv_sem, tile_send, tile_recv, own_sem, all_send, all_recv) = rest[8:]

    gx, gy = lax.axis_index("gx"), lax.axis_index("gy")
    me = gx * row + gy
    core = lax.rem(gy, 2)
    gz, yc, y = gy // 8, lax.rem(gy, 8), lax.rem(gy // 2, 4)

    def along_x(k):
        x = lax.rem(gx + k, 4)
        return x, (x, gy)

    def along_z(k):
        z = lax.rem(gz + k, 4)
        return z, (gx, z * 8 + yc)

    def along_yc(k):
        n = lax.rem(yc + k, 8)
        return n, (gx, gz * 8 + n)

    def along_y(k):
        n = lax.rem(y + k, 4)
        return n, (gx, gz * 8 + n * 2 + core)

    def device(d):
        d = lax.rem(d + devices, devices)
        return (d // row, lax.rem(d, row))

    peer = device(me + 1 - 2 * core)

    loads = [
        pltpu.make_async_copy(
            fields.at[:, :, :, pl.ds(q * 128, 128)], F.at[:, :, pl.ds(q * 32, 32), :], in_sem.at[q]
        )
        for q in range(8)
    ] + [
        pltpu.make_async_copy(
            speeds.at[:, :, :, pl.ds(q * 128, 128)],
            S.at[:, :, pl.ds(q * 32, 32), :],
            in_sem.at[8 + q],
        )
        for q in range(8)
    ]
    tile_load = pltpu.make_async_copy(tiles, TL, in_sem.at[16])
    for load in loads + [tile_load]:
        load.start()

    barrier = pltpu.get_barrier_semaphore()
    greeted = [device(me + offset) for offset in (-2, -1, 1, 2)]
    greeted += [along_x(k)[1] for k in (1, 2, 3)] + [along_z(k)[1] for k in (1, 2, 3)]
    greeted += [along_yc(k)[1] for k in range(1, 8)]
    for other in greeted:
        pl.semaphore_signal(barrier, inc=1, device_id=other, device_id_type=MESH)
    pl.semaphore_wait(barrier, len(greeted))

    def remote(src, dst, send, recv, target):
        return pltpu.make_async_remote_copy(
            src_ref=src, dst_ref=dst, send_sem=send, recv_sem=recv,
            device_id=target, device_id_type=MESH,
        )

    class Exchange:
        def __init__(self, slot_at, send, recv):
            self.at, self.send, self.recv = slot_at, send, recv

        def start(self):
            own = self.at(2)
            self.far_up = remote(own, self.at(0), self.send.at[0], self.recv.at[0], device(me + 2))
            self.far_down = remote(
                own, self.at(4), self.send.at[1], self.recv.at[4], device(me - 2)
            )
            near = 1 + 2 * core
            self.near = remote(own, self.at(near), self.send.at[2], self.recv.at[near], peer)
            self.far_up.start()
            self.far_down.start()
            self.near.start()

        def forward(self):
            self.got(0)
            self.got(4)
            source, target = 4 - 4 * core, 3 - 2 * core
            self.passed = remote(
                self.at(source), self.at(target), self.send.at[3], self.recv.at[target], peer
            )
            self.passed.start()

        def got(self, slot):
            remote(
                self.at(slot), self.at(slot), self.send.at[0], self.recv.at[slot], peer
            ).wait_recv()

        def finish(self):
            self.got(1)
            self.got(3)

        def sent(self):
            for copy in (self.far_up, self.far_down, self.near, self.passed):
                copy.wait_send()

    def pairs(pool):
        return lambda slot: pool.at[pl.ds(2 * slot, 2)]

    def single(pool):
        return lambda slot: pool.at[slot]

    faces = [
        [
            Exchange(
                single(pools[s][f]) if s == 1 else pairs(pools[s][f]),
                face_send.at[s, f],
                face_recv.at[s, f],
            )
            for f in range(NF)
        ]
        for s in range(3)
    ]
    winds = [
        Exchange(at, sp_send.at[s], sp_recv.at[s])
        for s, at in enumerate((pairs(SP0), single(SP1), pairs(SP2)))
    ]

    sub = lax.broadcasted_iota(jnp.int32, (8, 128), 0)
    lane = lax.broadcasted_iota(jnp.int32, (8, 128), 1)

    def place(n, reach):
        found = (jnp.right_shift(n, 1) - me + reach) * 2 + jnp.bitwise_and(n, 1)
        return jnp.minimum(jnp.maximum(found, 0), 4 * reach + 1)

    def spot(b, d, h):
        return place(neighbours[2 * d + h, me * NB + b], 2)

    def linked(b, d, h):
        return (neighbours[2 * d + h, me * NB + b] >= 0).astype(jnp.int32)

    def pack_rows(s, f, A):
        pool = pools[s][f]
        for b in range(NB):
            for m in range(3):
                pool[4 + b, m] = A[b, f, pl.ds(m, 8, stride=32), :]
                pool[4 + b, 3 + m] = A[b, f, pl.ds(29 + m, 8, stride=32), :]

    def shift_up(x, ghost):
        return jnp.where(sub == 7, ghost, pltpu.roll(x, 7, 0))

    def shift_down(x, ghost):
        return jnp.where(sub == 0, ghost, pltpu.roll(x, 1, 0))

    def coef_rows(A, index, SP, d, C):
        def step(it, carry):
            b, c = it // 8, lax.rem(it, 8)
            base = c * 32
            own = [A[b, index, pl.ds(base + r, 8, stride=4), :] for r in range(4)]
            edge = A[b, index, pl.ds(base + 31, 1), :]
            ghost = SP[spot(b, d, 1), pl.ds(c, 1), :]
            ghost = chosen(linked(b, d, 1), (1, 128), ghost, edge)
            for r, value in enumerate(own + [shift_up(own[0], ghost)]):
                for n, part in enumerate(coefficients(value)):
                    C[it, 3 * r + n] = part
            return carry

        lax.fori_loop(0, 16, step, 0, unroll=2)

    def sweep_rows(s, f, A, C, strided):
        pool = pools[s][f]

        def step(it, carry):
            b, c = it // 8, lax.rem(it, 8)
            base = pl.multiple_of(c * 32, 32)
            own = [A[b, f, pl.ds(base + r, 8, stride=4), :] for r in range(4)]
            low_edge = A[b, f, pl.ds(base, 1), :]
            high_edge = A[b, f, pl.ds(base + 31, 1), :]
            low, high = spot(b, s, 0), spot(b, s, 1)
            low_on, high_on = linked(b, s, 0), linked(b, s, 1)
            before, after = [], []
            for m in range(3):
                ghost = chosen(low_on, (1, 128), pool[low, 3 + m, pl.ds(c, 1), :], low_edge)
                before.append(shift_down(own[m + 1], ghost))
                ghost = chosen(high_on, (1, 128), pool[high, m, pl.ds(c, 1), :], high_edge)
                after.append(shift_up(own[m], ghost))
            courant = [[C[it, 3 * r + n] for n in range(3)] for r in range(5)]
            result = ppm(before + own + after, courant)
            for r in range(4):
                if strided:
                    A[b, f, pl.ds(base + r, 8, stride=4), :] = result[r]
                else:
                    A[b, f, pl.ds(base + 8 * r, 8), :] = result[r]
            return carry

        lax.fori_loop(0, 16, step, 0, unroll=4)

    def pack_side(f):
        pool = pools[1][f]
        for o in range(4):
            at = o * 8
            for m in range(3):
                low = [T[b, f, pl.ds(m * 32 + at, 8), :] for b in range(NB)]
                high = [T[b, f, pl.ds(128 + (m + 1) * 32 + at, 8), :] for b in range(NB)]
                pool[2, m, pl.ds(at, 8), :] = jnp.where(
                    lane < 64,
                    jnp.where(lane < 32, low[0], pltpu.roll(low[1], 32, 1)),
                    jnp.where(lane >= 96, high[0], pltpu.roll(high[1], 96, 1)),
                )

    def side_rows(A, b, n, at):
        return [A[b, n, pl.ds(r * 32 + at, 8), :] for r in range(8)]

    def before_first(ghost, second):
        return chosen(second, (8, 128), pltpu.roll(ghost, 64, 1), pltpu.roll(ghost, 32, 1))

    def after_last(ghost, second):
        return chosen(second, (8, 128), pltpu.roll(ghost, 64, 1), pltpu.roll(ghost, 96, 1))

    def coef_side():
        def step(it, carry):
            b, o = it // 4, lax.rem(it, 4)
            at = pl.multiple_of(o * 8, 8)
            own = side_rows(ST, b, 0, at)
            where = spot(b, 1, 1)
            ghost = after_last(SP1[where // 2, pl.ds(at, 8), :], lax.rem(where, 2))
            ghost = chosen(linked(b, 1, 1), (8, 128), ghost, own[7])
            own.append(jnp.where(lane >= 96, ghost, pltpu.roll(own[0], 96, 1)))
            for r, value in enumerate(own):
                for n, part in enumerate(coefficients(value)):
                    C1[it, 3 * r + n] = part
            return carry

        lax.fori_loop(0, 8, step, 0, unroll=2)

    def sweep_side(f):
        pool = pools[1][f]

        def step(it, carry):
            b, o = it // 4, lax.rem(it, 4)
            at = pl.multiple_of(o * 8, 8)
            own = side_rows(T, b, f, at)
            low, high = spot(b, 1, 0), spot(b, 1, 1)
            low_on, high_on = linked(b, 1, 0), linked(b, 1, 1)
            before, after = [], []
            for m in range(3):
                ghost = before_first(pool[low // 2, m, pl.ds(at, 8), :], lax.rem(low, 2))
                ghost = chosen(low_on, (8, 128), ghost, own[0])
                before.append(jnp.where(lane < 32, ghost, pltpu.roll(own[5 + m], 32, 1)))
                ghost = after_last(pool[high // 2, m, pl.ds(at, 8), :], lax.rem(high, 2))
                ghost = chosen(high_on, (8, 128), ghost, own[7])
                after.append(jnp.where(lane >= 96, ghost, pltpu.roll(own[m], 96, 1)))
            courant = [[C1[it, 3 * r + n] for n in range(3)] for r in range(9)]
            result = ppm(before + own + after, courant)
            for r in range(8):
                T[b, f, pl.ds(r * 32 + at, 8), :] = result[r]
            return carry

        lax.fori_loop(0, 8, step, 0, unroll=2)

    def turn(f):
        def step(it, carry):
            b, e = it // 2, lax.rem(it, 2)
            rows = [F[b, f, pl.ds((2 * q + e) * 32, 32), :] for q in range(4)]
            T[b, f, pl.ds(e * 128, 128), :] = jnp.concatenate(rows, axis=0).T
            return carry

        lax.fori_loop(0, 4, step, 0, unroll=4)

    def turn_speeds():
        for n in range(2):
            def step(it, carry):
                b, e = it // 2, lax.rem(it, 2)
                rows = [
                    S[b, n + 1, pl.ds((2 * q + e) * 32 + r, 8, stride=4), :]
                    for q in range(4)
                    for r in range(4)
                ]
                ST[b, n, pl.ds(e * 128, 128), :] = jnp.concatenate(rows, axis=0).T
                return carry

            lax.fori_loop(0, 4, step, 0, unroll=4)

    def turn_back(f):
        def step(it, carry):
            b, e = it // 2, lax.rem(it, 2)
            back = T[b, f, pl.ds(pl.multiple_of(e * 128, 128), 128), :].T
            for q in range(4):
                for r in range(4):
                    R[f][2 + b, pl.ds((2 * q + e) * 32 + r, 8, stride=4), :] = back[
                        q * 32 + r * 8 : q * 32 + r * 8 + 8
                    ]
            return carry

        lax.fori_loop(0, 4, step, 0, unroll=4)

    def find_tiles():
        t = lax.broadcasted_iota(jnp.int32, (128, 128), 0)
        p = lax.broadcasted_iota(jnp.int32, (128, 128), 1)
        dests = jnp.broadcast_to(dest[...], (128, 128)).T
        fills = jnp.broadcast_to(fill[...], (128, 128)).T
        match = dests == p

        def rows(x):
            return jnp.concatenate([x] * 16, axis=0)

        first = tree(jnp.minimum, jnp.where(match, t, 128))
        last = tree(jnp.maximum, jnp.where(match, t, -1))
        second = jnp.where(last > first, last, 128)
        first_fill = tree(jnp.add, jnp.where(t == rows(first), fills, 0))
        second_fill = tree(jnp.add, jnp.where(t == rows(second), fills, 0))
        where = jnp.where(sub == 0, jnp.minimum(first, 127), jnp.minimum(second, 127))
        INV[...] = jnp.where(sub < 2, where, jnp.where(sub == 2, first_fill, second_fill))
        G[me, 0:1] = first_fill[0:1]
        G[me, 1:2] = second_fill[0:1]
        copy = pltpu.make_async_copy(INV, INVS, inv_sem)
        copy.start()
        return copy

    def pack_tiles():
        def step(i, carry):
            for n in range(8):
                for h in range(CAPT):
                    x = TL[INVS[h, i * 8 + n]]
                    moved = jnp.where(sub < 3, x + DRIFT * pltpu.roll(x, 5, 0), x)
                    live = lane < jnp.full((8, 128), INVS[2 + h, i * 8 + n], jnp.int32)
                    B0[h][i // 4, lax.rem(i, 4), n] = jnp.where(live, moved, 0.0)
            return carry

        lax.fori_loop(0, 16, step, 0)

    class Part:
        def __init__(self, size, along, source, target, send, recv, own):
            here = along(0)[0]
            self.own = pltpu.make_async_copy(source(here), target(here), own)
            self.copies, self.arrivals = [], []
            for k in range(1, size):
                n, other = along(k)
                self.copies.append(remote(source(n), target(here), send.at[k], recv.at[k], other))
                n, other = along(size - k)
                self.arrivals.append(remote(source(n), target(n), send.at[k], recv.at[k], other))

        def start(self):
            for copy in self.copies:
                copy.start()
            self.own.start()

        def finish(self):
            self.own.wait()
            for copy in self.arrivals:
                copy.wait_recv()

        def sent(self):
            for copy in self.copies:
                copy.wait_send()

    def seen(ref, axis, n, *half):
        after = (slice(None),) * (2 - axis) if half else ()
        return ref.at[(slice(None),) * axis + (n,) + after + half]

    def part(h, phase):
        axis = ((0, 2, 1), (1, 0, 2))[h][phase]
        size, along = (4, 4, 8)[axis], (along_x, along_z, along_yc)[axis]
        source = (B0, B1, B2)[phase][h]
        target, half = (tiles_out, (h,)) if phase == 2 else ((B1, B2)[phase][h], ())
        return Part(
            size, along,
            lambda n: seen(source, axis, n), lambda n: seen(target, axis, n, *half),
            tile_send.at[h, phase], tile_recv.at[h, phase], own_sem.at[h, phase],
        )

    class Fills:
        def __init__(self, n):
            size = (1, 2, 8, 32)[n]
            base = me // size * size
            mine = G.at[pl.ds(base, size)]
            self.copies, self.arrivals = [], []
            for k in (1,) if n == 0 else (1, 2, 3):
                send, recv = all_send.at[n, k], all_recv.at[n, k]
                for list_, j in ((self.copies, k), (self.arrivals, (2 if n == 0 else 4) - k)):
                    if n == 0:
                        other, start = peer, me + 1 - 2 * core
                    else:
                        at, other = (along_y, along_z, along_x)[n - 1](j)
                        start = base + (at - (y, gz, gx)[n - 1]) * size
                    where = mine if list_ is self.copies else G.at[pl.ds(start, size)]
                    list_.append(remote(mine, where, send, recv, other))

        def start(self):
            for copy in self.copies:
                copy.start()

        def finish(self):
            for copy in self.arrivals:
                copy.wait_recv()

        sent = Part.sent

    parts = [[part(h, phase) for phase in range(3)] for h in range(CAPT)]
    fill_steps = [Fills(n) for n in range(4)]

    def own_fills():
        flat = lax.broadcasted_iota(jnp.int32, (2, 128), 0) * 128
        flat = flat + lax.broadcasted_iota(jnp.int32, (2, 128), 1)
        mine = lax.broadcasted_iota(jnp.int32, (2, 128), 1) == me

        def step(i, total):
            for n in range(8):
                source = i * 8 + n
                value = jnp.sum(jnp.where(mine, G[source], 0), axis=1, keepdims=True)
                for h in range(CAPT):
                    total = jnp.where(
                        flat == source * CAPT + h,
                        jnp.broadcast_to(value[h : h + 1], (2, 128)),
                        total,
                    )
            return total

        fill_out[...] = lax.fori_loop(0, 16, step, jnp.zeros((2, 128), jnp.int32))

    for load in loads:
        load.wait()
    for b in range(NB):
        SP0[4 + b] = S[b, 0, pl.ds(0, 8, stride=32), :]
    winds[0].start()
    for f in range(NF):
        pack_rows(0, f, F)
        faces[0][f].start()
    found = find_tiles()
    fill_steps[0].start()
    turn_speeds()
    found.wait()
    tile_load.wait()
    pack_tiles()
    queue = list(parts[0][0].copies)
    for n, copy in enumerate(parts[1][0].copies):
        queue.insert(3 * n, copy)
    for h in range(CAPT):
        parts[h][0].own.start()

    def tiles_at(t):
        for h in range(CAPT):
            for phase in range(2):
                if t == PHASE_AT[h][phase]:
                    parts[h][phase].finish()
                    parts[h][phase + 1].start()

    for b in range(NB):
        SP2[4 + b] = ST[b, 1, pl.ds(0, 8, stride=32), :]
    for o in range(4):
        at = o * 8
        SP1[2, pl.ds(at, 8), :] = jnp.where(
            lane < 32,
            ST[0, 0, pl.ds(at, 8), :],
            pltpu.roll(ST[1, 0, pl.ds(at, 8), :], 32, 1),
        )
    winds[1].start()
    winds[2].start()
    winds[0].forward()
    faces[0][0].forward()
    winds[0].finish()
    coef_rows(S, 0, SP0, 0, C0)

    moves = {}
    first_of = {s: min(t for t in range(3 * NF) if ORDER[t][0] == s) for s in range(3)}
    for t in range(3 * NF):
        s, f = ORDER[t]
        if t + 1 < 3 * NF:
            after_s, after_f = ORDER[t + 1]
            faces[after_s][after_f].forward()
        if t == 1:
            winds[1].forward()
            winds[2].forward()
        if t == first_of[1]:
            winds[1].finish()
            coef_side()
        if t == first_of[2]:
            winds[2].finish()
            coef_rows(ST, 1, SP2, 2, C2)
        if t in FILL_AT:
            n = FILL_AT.index(t)
            fill_steps[n].finish()
            fill_steps[n + 1].start()
        tiles_at(t)
        faces[s][f].finish()
        if s == 0:
            sweep_rows(0, f, F, C0, False)
            turn(f)
            pack_side(f)
            faces[1][f].start()
        elif s == 1:
            sweep_side(f)
            pack_rows(2, f, T)
            faces[2][f].start()
        else:
            sweep_rows(2, f, T, C2, True)
            turn_back(f)
            own = R[f].at[pl.ds(2, 2)]
            pair = [
                remote(own, R[f].at[pl.ds(0, 2)], mv_send.at[f, 0], mv_recv.at[f, 0], device(me + 1)),
                remote(own, R[f].at[pl.ds(4, 2)], mv_send.at[f, 1], mv_recv.at[f, 1], device(me - 1)),
            ]
            for copy in pair:
                copy.start()
            moves[f] = pair
        for _ in range(TILES_A_STEP):
            if queue:
                queue.pop(0).start()

    fill_steps[3].finish()
    own_fills()
    stores = []
    for f in range(NF):
        tiles_at(3 * NF + f)
        for copy in moves[f]:
            copy.wait_recv()
        for j in range(NB):
            def step(i, carry):
                at = pl.multiple_of(i * 8, 8)
                for q in range(8):
                    O[j, f, pl.ds(at, 8), pl.ds(q * 128, 128)] = R[f][
                        place(order[me * NB + j], 1), pl.ds(q * 32 + at, 8), :
                    ]
                return carry

            lax.fori_loop(0, 4, step, 0, unroll=2)
        stores.append(pltpu.make_async_copy(O.at[:, f], out.at[:, f], out_sem.at[f]))
        stores[-1].start()
    for h in range(CAPT):
        parts[h][2].finish()
    for group in faces + [winds, fill_steps] + parts:
        for exchange in group:
            exchange.sent()
    for pair in moves.values():
        for copy in pair:
            copy.wait_send()
    for store in stores:
        store.wait()


def advance(fields, speeds, neighbours, order, tiles, dest, fill, devices, row):
    f32, i32 = jnp.float32, jnp.int32
    dma = pltpu.SemaphoreType.DMA
    scratch = [
        pltpu.VMEM((NB, NF, 256, 128), f32),
        pltpu.VMEM((NB, 3, 256, 128), f32),
        pltpu.VMEM((NB, NF, 256, 128), f32),
        pltpu.VMEM((NB, 2, 256, 128), f32),
        pltpu.VMEM((NB, NF, 32, 1024), f32),
        pltpu.VMEM((10, 8, 128), f32),
        pltpu.VMEM((5, 32, 128), f32),
        pltpu.VMEM((10, 8, 128), f32),
    ]
    scratch += [pltpu.VMEM((8, 27, 8, 128) if s == 1 else (16, 15, 8, 128), f32) for s in range(3)]
    for s in range(3):
        shape = (5, 3, 32, 128) if s == 1 else (10, 6, 8, 128)
        scratch += [pltpu.VMEM(shape, f32) for _ in range(NF)]
    scratch += [pltpu.VMEM((6, 256, 128), f32) for _ in range(NF)]
    scratch += [
        pltpu.VMEM((128, 8, 128), f32),
        pltpu.VMEM((128, CAPT, 128), i32),
        pltpu.VMEM((8, 128), i32),
        pltpu.SMEM((8, 128), i32),
    ]
    scratch += [pltpu.VMEM((4, 4, 8, 8, 128), f32) for _ in range(3 * CAPT)]
    scratch += [
        dma((17,)), dma((3, NF, 4)), dma((3, NF, 5)), dma((3, 4)), dma((3, 5)),
        dma((NF, 2)), dma((NF, 2)), dma((NF,)),
        dma(()), dma((CAPT, 3, 8)), dma((CAPT, 3, 8)), dma((CAPT, 3)), dma((4, 4)), dma((4, 4)),
    ]
    return pl.pallas_call(
        functools.partial(advance_kernel, devices, row),
        out_shape=(
            jax.ShapeDtypeStruct(fields.shape, f32),
            jax.ShapeDtypeStruct((4, 4, 8, CAPT, 8, 128), f32),
            jax.ShapeDtypeStruct((CAPT, 128), i32),
        ),
        in_specs=[
            pl.BlockSpec(memory_space=pltpu.SMEM),
            pl.BlockSpec(memory_space=pltpu.SMEM),
            pl.BlockSpec(memory_space=pltpu.HBM),
            pl.BlockSpec(memory_space=pltpu.HBM),
            pl.BlockSpec(memory_space=pltpu.HBM),
            pl.BlockSpec(memory_space=pltpu.VMEM),
            pl.BlockSpec(memory_space=pltpu.VMEM),
        ],
        out_specs=(
            pl.BlockSpec(memory_space=pl.ANY),
            pl.BlockSpec(memory_space=pl.ANY),
            pl.BlockSpec(memory_space=pltpu.VMEM),
        ),
        scratch_shapes=scratch,
        name="advance_blocks",
        compiler_params=pltpu.CompilerParams(
            collective_id=0, has_side_effects=True, vmem_limit_bytes=60 * 1024 * 1024
        ),
    )(neighbours, order, fields, speeds, tiles, dest, fill)


def body(fields, speeds, neighbours, block_order, tiles, tile_fill, tile_dest):
    row = lax.axis_size("gy")
    devices = lax.axis_size(AXES)
    blocks_out, tiles_out, fill_out = advance(
        fields, speeds, neighbours.T, block_order, tiles,
        tile_dest.reshape(1, -1), tile_fill.reshape(1, -1), devices, row,
    )
    return blocks_out, tiles_out.reshape((-1,) + tiles.shape[1:]), fill_out.reshape(-1)


def solution(mesh):
    blocks = P(AXES, None, None, None)
    return jax.shard_map(
        body,
        mesh=mesh,
        in_specs=(blocks, blocks, P(), P(), P(AXES, None, None), P(AXES), P(AXES, None)),
        out_specs=(blocks, P(AXES, None, None), P(AXES)),
        check_vma=False,
    )
```

```python
import functools

import jax
import jax.numpy as jnp
from jax import lax
from jax.experimental import pallas as pl
from jax.experimental.pallas import tpu as pltpu
from jax.sharding import PartitionSpec as P

MESH = pl.DeviceIdType.MESH
NF = 6
NB = 2
CAPT = 2
DRIFT = 0.5
AXES = ("gx", "gy")


def ppm(cells, courant):
    n = len(cells) - 6
    delta = [cells[i + 1] - cells[i] for i in range(n + 5)]
    right, left = {}, {}
    for i in range(1, n + 4):
        step = 0.5 * delta[i] + (1.0 / 12.0) * (delta[i - 1] - delta[i + 1])
        step = jnp.minimum(
            jnp.maximum(step, jnp.minimum(delta[i], 0.0)), jnp.maximum(delta[i], 0.0)
        )
        right[i], left[i + 1] = step, delta[i] - step
    up, down = {}, {}
    for i in range(2, n + 4):
        r, l = right[i], left[i]
        r2, l2 = r + r, l + l
        up[i] = jnp.maximum(jnp.minimum(r, l2), 0.0) + jnp.minimum(jnp.maximum(r, l2), 0.0)
        down[i] = jnp.maximum(jnp.minimum(l, r2), 0.0) + jnp.minimum(jnp.maximum(l, r2), 0.0)
    flux = []
    for f in range(n + 1):
        c, ca, cb = courant[f]
        a, b = f + 2, f + 3
        wind = c > 0.0
        flux.append(
            c * jnp.where(wind, cells[a], cells[b])
            + ca * jnp.where(wind, up[a], down[b])
            + cb * jnp.where(wind, down[a], up[b])
        )
    return [cells[r + 3] - (flux[r + 1] - flux[r]) for r in range(n)]


def coefficients(c):
    size = jnp.abs(c)
    rest = 1.0 - size
    side = size * rest
    return c, side * rest, side * size


def chosen(flag, shape, ghost, edge):
    return jnp.where(jnp.full(shape, flag, jnp.int32) != 0, ghost, edge)


def tree(op, x):
    parts = [x[8 * i : 8 * i + 8] for i in range(16)]
    while len(parts) > 1:
        parts = [op(p, q) for p, q in zip(parts[::2], parts[1::2])]
    value = parts[0]
    for shift in (4, 2, 1):
        value = op(value, pltpu.roll(value, shift, 0))
    return value


FILL_AT = (2, 7, 12)
PHASE_AT = ((8, 15), (8, 15))
TILES_A_STEP = 3
ORDER = [(s, f) for s in range(3) for f in range(NF)]


def advance_kernel(devices, row, neighbours, order, fields, speeds, tiles, dest, fill, *refs):
    out, tiles_out, fill_out = refs[:3]
    (F, S, T, ST, O, SP0, SP1, SP2, C0, C1, C2), rest = refs[3:14], refs[14:]
    pools = [rest[6 * s : 6 * s + 6] for s in range(3)]
    R, rest = rest[18:24], rest[24:]
    (TL, G, INV, INVS), B0, B1, B2, rest = rest[:4], rest[4:6], rest[6:8], rest[8:10], rest[10:]
    (in_sem, face_send, face_recv, sp_send, sp_recv, mv_send, mv_recv, out_sem) = rest[:8]
    (inv_sem, tile_send, tile_recv, own_sem, all_send, all_recv) = rest[8:]

    gx, gy = lax.axis_index("gx"), lax.axis_index("gy")
    me = gx * row + gy
    core = lax.rem(gy, 2)
    gz, yc, y = gy // 8, lax.rem(gy, 8), lax.rem(gy // 2, 4)

    def along_x(k):
        x = lax.rem(gx + k, 4)
        return x, (x, gy)

    def along_z(k):
        z = lax.rem(gz + k, 4)
        return z, (gx, z * 8 + yc)

    def along_yc(k):
        n = lax.rem(yc + k, 8)
        return n, (gx, gz * 8 + n)

    def along_y(k):
        n = lax.rem(y + k, 4)
        return n, (gx, gz * 8 + n * 2 + core)

    def device(d):
        d = lax.rem(d + devices, devices)
        return (d // row, lax.rem(d, row))

    peer = device(me + 1 - 2 * core)

    loads = [
        pltpu.make_async_copy(
            fields.at[:, :, :, pl.ds(q * 128, 128)], F.at[:, :, pl.ds(q * 32, 32), :], in_sem.at[q]
        )
        for q in range(8)
    ] + [
        pltpu.make_async_copy(
            speeds.at[:, :, :, pl.ds(q * 128, 128)],
            S.at[:, :, pl.ds(q * 32, 32), :],
            in_sem.at[8 + q],
        )
        for q in range(8)
    ]
    tile_load = pltpu.make_async_copy(tiles, TL, in_sem.at[16])
    for load in loads + [tile_load]:
        load.start()

    barrier = pltpu.get_barrier_semaphore()
    greeted = [device(me + offset) for offset in (-2, -1, 1, 2)]
    greeted += [along_x(k)[1] for k in (1, 2, 3)] + [along_z(k)[1] for k in (1, 2, 3)]
    greeted += [along_yc(k)[1] for k in range(1, 8)]
    for other in greeted:
        pl.semaphore_signal(barrier, inc=1, device_id=other, device_id_type=MESH)
    pl.semaphore_wait(barrier, len(greeted))

    def remote(src, dst, send, recv, target):
        return pltpu.make_async_remote_copy(
            src_ref=src, dst_ref=dst, send_sem=send, recv_sem=recv,
            device_id=target, device_id_type=MESH,
        )

    class Exchange:
        def __init__(self, slot_at, send, recv):
            self.at, self.send, self.recv = slot_at, send, recv

        def start(self):
            own = self.at(2)
            self.far_up = remote(own, self.at(0), self.send.at[0], self.recv.at[0], device(me + 2))
            self.far_down = remote(
                own, self.at(4), self.send.at[1], self.recv.at[4], device(me - 2)
            )
            near = 1 + 2 * core
            self.near = remote(own, self.at(near), self.send.at[2], self.recv.at[near], peer)
            self.far_up.start()
            self.far_down.start()
            self.near.start()

        def forward(self):
            source, target = 4 - 4 * core, 3 - 2 * core
            self.got(source)
            self.passed = remote(
                self.at(source), self.at(target), self.send.at[3], self.recv.at[target], peer
            )
            self.passed.start()

        def got(self, slot):
            remote(
                self.at(slot), self.at(slot), self.send.at[0], self.recv.at[slot], peer
            ).wait_recv()

        def finish(self):
            self.got(4 * core)
            self.got(1)
            self.got(3)

        def sent(self):
            for copy in (self.far_up, self.far_down, self.near, self.passed):
                copy.wait_send()

    def pairs(pool):
        return lambda slot: pool.at[pl.ds(2 * slot, 2)]

    def single(pool):
        return lambda slot: pool.at[slot]

    faces = [
        [
            Exchange(
                single(pools[s][f]) if s == 1 else pairs(pools[s][f]),
                face_send.at[s, f],
                face_recv.at[s, f],
            )
            for f in range(NF)
        ]
        for s in range(3)
    ]
    winds = [
        Exchange(at, sp_send.at[s], sp_recv.at[s])
        for s, at in enumerate((pairs(SP0), single(SP1), pairs(SP2)))
    ]

    sub = lax.broadcasted_iota(jnp.int32, (8, 128), 0)
    lane = lax.broadcasted_iota(jnp.int32, (8, 128), 1)

    def place(n, reach):
        found = (jnp.right_shift(n, 1) - me + reach) * 2 + jnp.bitwise_and(n, 1)
        return jnp.minimum(jnp.maximum(found, 0), 4 * reach + 1)

    def spot(b, d, h):
        return place(neighbours[2 * d + h, me * NB + b], 2)

    def linked(b, d, h):
        return (neighbours[2 * d + h, me * NB + b] >= 0).astype(jnp.int32)

    def pack_rows(s, f, A):
        pool = pools[s][f]
        for b in range(NB):
            for m in range(3):
                pool[4 + b, m] = A[b, f, pl.ds(m, 8, stride=32), :]
                pool[4 + b, 3 + m] = A[b, f, pl.ds(29 + m, 8, stride=32), :]

    def shift_up(x, ghost):
        return jnp.where(sub == 7, ghost, pltpu.roll(x, 7, 0))

    def shift_down(x, ghost):
        return jnp.where(sub == 0, ghost, pltpu.roll(x, 1, 0))

    def coef_rows(A, index, SP, d, C):
        def step(it, carry):
            b, c = it // 8, lax.rem(it, 8)
            base = c * 32
            own = [A[b, index, pl.ds(base + r, 8, stride=4), :] for r in range(4)]
            edge = A[b, index, pl.ds(base + 31, 1), :]
            ghost = SP[spot(b, d, 1), pl.ds(c, 1), :]
            ghost = chosen(linked(b, d, 1), (1, 128), ghost, edge)
            for r, value in enumerate(own + [shift_up(own[0], ghost)]):
                for n, part in enumerate(coefficients(value)):
                    C[it, 3 * r + n] = part
            return carry

        lax.fori_loop(0, 16, step, 0, unroll=2)

    def sweep_rows(s, f, A, C, strided):
        pool = pools[s][f]

        def step(it, carry):
            b, c = it // 8, lax.rem(it, 8)
            base = pl.multiple_of(c * 32, 32)
            own = [A[b, f, pl.ds(base + r, 8, stride=4), :] for r in range(4)]
            low_edge = A[b, f, pl.ds(base, 1), :]
            high_edge = A[b, f, pl.ds(base + 31, 1), :]
            low, high = spot(b, s, 0), spot(b, s, 1)
            low_on, high_on = linked(b, s, 0), linked(b, s, 1)
            before, after = [], []
            for m in range(3):
                ghost = chosen(low_on, (1, 128), pool[low, 3 + m, pl.ds(c, 1), :], low_edge)
                before.append(shift_down(own[m + 1], ghost))
                ghost = chosen(high_on, (1, 128), pool[high, m, pl.ds(c, 1), :], high_edge)
                after.append(shift_up(own[m], ghost))
            courant = [[C[it, 3 * r + n] for n in range(3)] for r in range(5)]
            result = ppm(before + own + after, courant)
            for r in range(4):
                if strided:
                    A[b, f, pl.ds(base + r, 8, stride=4), :] = result[r]
                else:
                    A[b, f, pl.ds(base + 8 * r, 8), :] = result[r]
            return carry

        lax.fori_loop(0, 16, step, 0, unroll=4)

    def pack_side(f):
        pool = pools[1][f]
        for o in range(4):
            at = o * 8
            for m in range(3):
                low = [T[b, f, pl.ds(m * 32 + at, 8), :] for b in range(NB)]
                high = [T[b, f, pl.ds(128 + (m + 1) * 32 + at, 8), :] for b in range(NB)]
                pool[2, m, pl.ds(at, 8), :] = jnp.where(
                    lane < 64,
                    jnp.where(lane < 32, low[0], pltpu.roll(low[1], 32, 1)),
                    jnp.where(lane >= 96, high[0], pltpu.roll(high[1], 96, 1)),
                )

    def side_rows(A, b, n, at):
        return [A[b, n, pl.ds(r * 32 + at, 8), :] for r in range(8)]

    def before_first(ghost, second):
        return chosen(second, (8, 128), pltpu.roll(ghost, 64, 1), pltpu.roll(ghost, 32, 1))

    def after_last(ghost, second):
        return chosen(second, (8, 128), pltpu.roll(ghost, 64, 1), pltpu.roll(ghost, 96, 1))

    def coef_side():
        def step(it, carry):
            b, o = it // 4, lax.rem(it, 4)
            at = pl.multiple_of(o * 8, 8)
            own = side_rows(ST, b, 0, at)
            where = spot(b, 1, 1)
            ghost = after_last(SP1[where // 2, pl.ds(at, 8), :], lax.rem(where, 2))
            ghost = chosen(linked(b, 1, 1), (8, 128), ghost, own[7])
            own.append(jnp.where(lane >= 96, ghost, pltpu.roll(own[0], 96, 1)))
            for r, value in enumerate(own):
                for n, part in enumerate(coefficients(value)):
                    C1[it, 3 * r + n] = part
            return carry

        lax.fori_loop(0, 8, step, 0, unroll=2)

    def sweep_side(f):
        pool = pools[1][f]

        def step(it, carry):
            b, o = it // 4, lax.rem(it, 4)
            at = pl.multiple_of(o * 8, 8)
            own = side_rows(T, b, f, at)
            low, high = spot(b, 1, 0), spot(b, 1, 1)
            low_on, high_on = linked(b, 1, 0), linked(b, 1, 1)
            before, after = [], []
            for m in range(3):
                ghost = before_first(pool[low // 2, m, pl.ds(at, 8), :], lax.rem(low, 2))
                ghost = chosen(low_on, (8, 128), ghost, own[0])
                before.append(jnp.where(lane < 32, ghost, pltpu.roll(own[5 + m], 32, 1)))
                ghost = after_last(pool[high // 2, m, pl.ds(at, 8), :], lax.rem(high, 2))
                ghost = chosen(high_on, (8, 128), ghost, own[7])
                after.append(jnp.where(lane >= 96, ghost, pltpu.roll(own[m], 96, 1)))
            courant = [[C1[it, 3 * r + n] for n in range(3)] for r in range(9)]
            result = ppm(before + own + after, courant)
            for r in range(8):
                T[b, f, pl.ds(r * 32 + at, 8), :] = result[r]
            return carry

        lax.fori_loop(0, 8, step, 0, unroll=2)

    def turn(f):
        def step(it, carry):
            b, e = it // 2, lax.rem(it, 2)
            rows = [F[b, f, pl.ds((2 * q + e) * 32, 32), :] for q in range(4)]
            T[b, f, pl.ds(e * 128, 128), :] = jnp.concatenate(rows, axis=0).T
            return carry

        lax.fori_loop(0, 4, step, 0, unroll=4)

    def turn_speeds():
        for n in range(2):
            def step(it, carry):
                b, e = it // 2, lax.rem(it, 2)
                rows = [
                    S[b, n + 1, pl.ds((2 * q + e) * 32 + r, 8, stride=4), :]
                    for q in range(4)
                    for r in range(4)
                ]
                ST[b, n, pl.ds(e * 128, 128), :] = jnp.concatenate(rows, axis=0).T
                return carry

            lax.fori_loop(0, 4, step, 0, unroll=4)

    def turn_back(f):
        def step(it, carry):
            b, e = it // 2, lax.rem(it, 2)
            back = T[b, f, pl.ds(pl.multiple_of(e * 128, 128), 128), :].T
            for q in range(4):
                for r in range(4):
                    R[f][2 + b, pl.ds((2 * q + e) * 32 + r, 8, stride=4), :] = back[
                        q * 32 + r * 8 : q * 32 + r * 8 + 8
                    ]
            return carry

        lax.fori_loop(0, 4, step, 0, unroll=4)

    def find_tiles():
        t = lax.broadcasted_iota(jnp.int32, (128, 128), 0)
        p = lax.broadcasted_iota(jnp.int32, (128, 128), 1)
        dests = jnp.broadcast_to(dest[...], (128, 128)).T
        fills = jnp.broadcast_to(fill[...], (128, 128)).T
        match = dests == p

        def rows(x):
            return jnp.concatenate([x] * 16, axis=0)

        first = tree(jnp.minimum, jnp.where(match, t, 128))
        last = tree(jnp.maximum, jnp.where(match, t, -1))
        second = jnp.where(last > first, last, 128)
        first_fill = tree(jnp.add, jnp.where(t == rows(first), fills, 0))
        second_fill = tree(jnp.add, jnp.where(t == rows(second), fills, 0))
        where = jnp.where(sub == 0, jnp.minimum(first, 127), jnp.minimum(second, 127))
        INV[...] = jnp.where(sub < 2, where, jnp.where(sub == 2, first_fill, second_fill))
        G[me, 0:1] = first_fill[0:1]
        G[me, 1:2] = second_fill[0:1]
        copy = pltpu.make_async_copy(INV, INVS, inv_sem)
        copy.start()
        return copy

    def pack_tiles():
        def step(i, carry):
            for n in range(8):
                for h in range(CAPT):
                    x = TL[INVS[h, i * 8 + n]]
                    moved = jnp.where(sub < 3, x + DRIFT * pltpu.roll(x, 5, 0), x)
                    live = lane < jnp.full((8, 128), INVS[2 + h, i * 8 + n], jnp.int32)
                    B0[h][i // 4, lax.rem(i, 4), n] = jnp.where(live, moved, 0.0)
            return carry

        lax.fori_loop(0, 16, step, 0)

    class Part:
        def __init__(self, size, along, source, target, send, recv, own):
            here = along(0)[0]
            self.own = pltpu.make_async_copy(source(here), target(here), own)
            self.copies, self.arrivals = [], []
            for k in range(1, size):
                n, other = along(k)
                self.copies.append(remote(source(n), target(here), send.at[k], recv.at[k], other))
                n, other = along(size - k)
                self.arrivals.append(remote(source(n), target(n), send.at[k], recv.at[k], other))

        def start(self):
            for copy in self.copies:
                copy.start()
            self.own.start()

        def finish(self):
            self.own.wait()
            for copy in self.arrivals:
                copy.wait_recv()

        def sent(self):
            for copy in self.copies:
                copy.wait_send()

    def seen(ref, axis, n, *half):
        after = (slice(None),) * (2 - axis) if half else ()
        return ref.at[(slice(None),) * axis + (n,) + after + half]

    def part(h, phase):
        axis = ((0, 2, 1), (1, 0, 2))[h][phase]
        size, along = (4, 4, 8)[axis], (along_x, along_z, along_yc)[axis]
        source = (B0, B1, B2)[phase][h]
        target, half = (tiles_out, (h,)) if phase == 2 else ((B1, B2)[phase][h], ())
        return Part(
            size, along,
            lambda n: seen(source, axis, n), lambda n: seen(target, axis, n, *half),
            tile_send.at[h, phase], tile_recv.at[h, phase], own_sem.at[h, phase],
        )

    class Fills:
        def __init__(self, n):
            size = (1, 2, 8, 32)[n]
            base = me // size * size
            mine = G.at[pl.ds(base, size)]
            self.copies, self.arrivals = [], []
            for k in (1,) if n == 0 else (1, 2, 3):
                send, recv = all_send.at[n, k], all_recv.at[n, k]
                for list_, j in ((self.copies, k), (self.arrivals, (2 if n == 0 else 4) - k)):
                    if n == 0:
                        other, start = peer, me + 1 - 2 * core
                    else:
                        at, other = (along_y, along_z, along_x)[n - 1](j)
                        start = base + (at - (y, gz, gx)[n - 1]) * size
                    where = mine if list_ is self.copies else G.at[pl.ds(start, size)]
                    list_.append(remote(mine, where, send, recv, other))

        def start(self):
            for copy in self.copies:
                copy.start()

        def finish(self):
            for copy in self.arrivals:
                copy.wait_recv()

        sent = Part.sent

    parts = [[part(h, phase) for phase in range(3)] for h in range(CAPT)]
    fill_steps = [Fills(n) for n in range(4)]

    def own_fills():
        flat = lax.broadcasted_iota(jnp.int32, (2, 128), 0) * 128
        flat = flat + lax.broadcasted_iota(jnp.int32, (2, 128), 1)
        mine = lax.broadcasted_iota(jnp.int32, (2, 128), 1) == me

        def step(i, total):
            for n in range(8):
                source = i * 8 + n
                value = jnp.sum(jnp.where(mine, G[source], 0), axis=1, keepdims=True)
                for h in range(CAPT):
                    total = jnp.where(
                        flat == source * CAPT + h,
                        jnp.broadcast_to(value[h : h + 1], (2, 128)),
                        total,
                    )
            return total

        fill_out[...] = lax.fori_loop(0, 16, step, jnp.zeros((2, 128), jnp.int32))

    for load in loads:
        load.wait()
    for b in range(NB):
        SP0[4 + b] = S[b, 0, pl.ds(0, 8, stride=32), :]
    winds[0].start()
    for f in range(NF):
        pack_rows(0, f, F)
        faces[0][f].start()
    found = find_tiles()
    fill_steps[0].start()
    turn_speeds()
    found.wait()
    tile_load.wait()
    pack_tiles()
    queue = list(parts[0][0].copies)
    for n, copy in enumerate(parts[1][0].copies):
        queue.insert(3 * n, copy)
    for h in range(CAPT):
        parts[h][0].own.start()

    def tiles_at(t):
        for h in range(CAPT):
            for phase in range(2):
                if t == PHASE_AT[h][phase]:
                    parts[h][phase].finish()
                    parts[h][phase + 1].start()

    for b in range(NB):
        SP2[4 + b] = ST[b, 1, pl.ds(0, 8, stride=32), :]
    for o in range(4):
        at = o * 8
        SP1[2, pl.ds(at, 8), :] = jnp.where(
            lane < 32,
            ST[0, 0, pl.ds(at, 8), :],
            pltpu.roll(ST[1, 0, pl.ds(at, 8), :], 32, 1),
        )
    winds[1].start()
    winds[2].start()
    winds[0].forward()
    faces[0][0].forward()
    winds[0].finish()
    coef_rows(S, 0, SP0, 0, C0)

    moves = {}
    first_of = {s: min(t for t in range(3 * NF) if ORDER[t][0] == s) for s in range(3)}
    for t in range(3 * NF):
        s, f = ORDER[t]
        if t + 1 < 3 * NF:
            after_s, after_f = ORDER[t + 1]
            faces[after_s][after_f].forward()
        if t == 1:
            winds[1].forward()
            winds[2].forward()
        if t == first_of[1]:
            winds[1].finish()
            coef_side()
        if t == first_of[2]:
            winds[2].finish()
            coef_rows(ST, 1, SP2, 2, C2)
        if t in FILL_AT:
            n = FILL_AT.index(t)
            fill_steps[n].finish()
            fill_steps[n + 1].start()
        tiles_at(t)
        faces[s][f].finish()
        if s == 0:
            sweep_rows(0, f, F, C0, False)
            turn(f)
            pack_side(f)
            faces[1][f].start()
        elif s == 1:
            sweep_side(f)
            pack_rows(2, f, T)
            faces[2][f].start()
        else:
            sweep_rows(2, f, T, C2, True)
            turn_back(f)
            own = R[f].at[pl.ds(2, 2)]
            pair = [
                remote(own, R[f].at[pl.ds(0, 2)], mv_send.at[f, 0], mv_recv.at[f, 0], device(me + 1)),
                remote(own, R[f].at[pl.ds(4, 2)], mv_send.at[f, 1], mv_recv.at[f, 1], device(me - 1)),
            ]
            for copy in pair:
                copy.start()
            moves[f] = pair
        for _ in range(TILES_A_STEP):
            if queue:
                queue.pop(0).start()

    fill_steps[3].finish()
    own_fills()
    stores = []
    for f in range(NF):
        tiles_at(3 * NF + f)
        for copy in moves[f]:
            copy.wait_recv()
        for j in range(NB):
            def step(i, carry):
                at = pl.multiple_of(i * 8, 8)
                for q in range(8):
                    O[j, f, pl.ds(at, 8), pl.ds(q * 128, 128)] = R[f][
                        place(order[me * NB + j], 1), pl.ds(q * 32 + at, 8), :
                    ]
                return carry

            lax.fori_loop(0, 4, step, 0, unroll=2)
        stores.append(pltpu.make_async_copy(O.at[:, f], out.at[:, f], out_sem.at[f]))
        stores[-1].start()
    for h in range(CAPT):
        parts[h][2].finish()
    for group in faces + [winds, fill_steps] + parts:
        for exchange in group:
            exchange.sent()
    for pair in moves.values():
        for copy in pair:
            copy.wait_send()
    for store in stores:
        store.wait()


def advance(fields, speeds, neighbours, order, tiles, dest, fill, devices, row):
    f32, i32 = jnp.float32, jnp.int32
    dma = pltpu.SemaphoreType.DMA
    scratch = [
        pltpu.VMEM((NB, NF, 256, 128), f32),
        pltpu.VMEM((NB, 3, 256, 128), f32),
        pltpu.VMEM((NB, NF, 256, 128), f32),
        pltpu.VMEM((NB, 2, 256, 128), f32),
        pltpu.VMEM((NB, NF, 32, 1024), f32),
        pltpu.VMEM((10, 8, 128), f32),
        pltpu.VMEM((5, 32, 128), f32),
        pltpu.VMEM((10, 8, 128), f32),
    ]
    scratch += [pltpu.VMEM((8, 27, 8, 128) if s == 1 else (16, 15, 8, 128), f32) for s in range(3)]
    for s in range(3):
        shape = (5, 3, 32, 128) if s == 1 else (10, 6, 8, 128)
        scratch += [pltpu.VMEM(shape, f32) for _ in range(NF)]
    scratch += [pltpu.VMEM((6, 256, 128), f32) for _ in range(NF)]
    scratch += [
        pltpu.VMEM((128, 8, 128), f32),
        pltpu.VMEM((128, CAPT, 128), i32),
        pltpu.VMEM((8, 128), i32),
        pltpu.SMEM((8, 128), i32),
    ]
    scratch += [pltpu.VMEM((4, 4, 8, 8, 128), f32) for _ in range(3 * CAPT)]
    scratch += [
        dma((17,)), dma((3, NF, 4)), dma((3, NF, 5)), dma((3, 4)), dma((3, 5)),
        dma((NF, 2)), dma((NF, 2)), dma((NF,)),
        dma(()), dma((CAPT, 3, 8)), dma((CAPT, 3, 8)), dma((CAPT, 3)), dma((4, 4)), dma((4, 4)),
    ]
    return pl.pallas_call(
        functools.partial(advance_kernel, devices, row),
        out_shape=(
            jax.ShapeDtypeStruct(fields.shape, f32),
            jax.ShapeDtypeStruct((4, 4, 8, CAPT, 8, 128), f32),
            jax.ShapeDtypeStruct((CAPT, 128), i32),
        ),
        in_specs=[
            pl.BlockSpec(memory_space=pltpu.SMEM),
            pl.BlockSpec(memory_space=pltpu.SMEM),
            pl.BlockSpec(memory_space=pltpu.HBM),
            pl.BlockSpec(memory_space=pltpu.HBM),
            pl.BlockSpec(memory_space=pltpu.HBM),
            pl.BlockSpec(memory_space=pltpu.VMEM),
            pl.BlockSpec(memory_space=pltpu.VMEM),
        ],
        out_specs=(
            pl.BlockSpec(memory_space=pl.ANY),
            pl.BlockSpec(memory_space=pl.ANY),
            pl.BlockSpec(memory_space=pltpu.VMEM),
        ),
        scratch_shapes=scratch,
        name="advance_blocks",
        compiler_params=pltpu.CompilerParams(
            collective_id=0, has_side_effects=True, vmem_limit_bytes=60 * 1024 * 1024
        ),
    )(neighbours, order, fields, speeds, tiles, dest, fill)


def body(fields, speeds, neighbours, block_order, tiles, tile_fill, tile_dest):
    row = lax.axis_size("gy")
    devices = lax.axis_size(AXES)
    blocks_out, tiles_out, fill_out = advance(
        fields, speeds, neighbours.T, block_order, tiles,
        tile_dest.reshape(1, -1), tile_fill.reshape(1, -1), devices, row,
    )
    return blocks_out, tiles_out.reshape((-1,) + tiles.shape[1:]), fill_out.reshape(-1)


def solution(mesh):
    blocks = P(AXES, None, None, None)
    return jax.shard_map(
        body,
        mesh=mesh,
        in_specs=(blocks, blocks, P(), P(), P(AXES, None, None), P(AXES), P(AXES, None)),
        out_specs=(blocks, P(AXES, None, None), P(AXES)),
        check_vma=False,
    )
```
